32 devices in a mesh: parts: 2 (over x), row: 16 (over z, y, core).
Axes of the slice: x: 2, y: 2, z: 4, core: 2. Of those that a mesh axis runs over, the one named last changes fastest.
Arguments:
- pair: bfloat16 [512, 256, 128], P(('parts', 'row')), parts along dimension 0, may hold values from -6 to 6
- pair_mask: int32 [512, 256], P(('parts', 'row')), parts along dimension 0, may hold values 0 or 1
- in_gain: float32 [128], replicated, may hold values from 0.1 to 1.9
- in_proj: bfloat16 [128, 512], replicated, may hold values from -0.5 to 0.5
- gate_proj: bfloat16 [128, 128], replicated, may hold values from -0.5 to 0.5
- out_proj: bfloat16 [128, 128], replicated, may hold values from -0.5 to 0.5
Outputs:
- update: bfloat16 [512, 256, 128], P(('parts', 'row')), parts along dimension 0
The draws below stay inside these ranges and needn't reach their ends.
There are 2 independent parts, one for each index of `parts`. The reference program is written for one: setup_inputs(seed, part) draws one part's arguments, and reference() takes and returns one part's arrays. A program takes and returns all parts, laid end to end along the dimension named above; an argument that names none is the same for every part. Nothing has to cross between parts.
All inputs are finite; a program needn't handle non-finite values. No bound on the sum of `pair_mask` on one device may be relied on, other than what follows from the above.
Results may differ from the reference program's by a relative error of at most 0.0085.
Values may be sent and summed in bfloat16 or wider, within the bound.
No kernel may reach another device: no remote copies, remote signals or barrier semaphores. Data moves between devices by JAX's collectives and lax.ppermute only.
A program may use at most 128 MiB of HBM per device.

```python
import jax
import jax.numpy as jnp
from jax import lax

D = 128
CH = 128
N = 256


def set_ends(values, rng, least, top_value):
    spot = [jax.random.randint(jax.random.fold_in(rng, axis), (), 0, length) for axis, length in enumerate(values.shape)]
    longest = values.shape.index(max(values.shape))
    neighbour = spot[:longest] + [(spot[longest] + 1) % values.shape[longest]] + spot[longest + 1:]
    return values.at[tuple(spot)].set(least).at[tuple(neighbour)].set(top_value)


def steps_of(stream_key, extent, pieces, least, top_value):
    factor_of, own = 1.0, jax.random.fold_in(stream_key, 6)
    for axis_at, shards_of in pieces:
        heights = jnp.exp(jax.random.uniform(jax.random.fold_in(own, axis_at), (shards_of,), jnp.float32, least / len(pieces), top_value / len(pieces)))
        factor_of = factor_of * jnp.repeat(heights, extent[axis_at] // shards_of).reshape([-1 if axis == axis_at else 1 for axis in range(len(extent))])
    return factor_of


def normal_values(rng, extent, scale, limit, split=(), dtype=jnp.bfloat16):
    drawn = scale * jax.random.normal(rng, extent, jnp.float32)
    if split:
        drawn = drawn * steps_of(rng, extent, split, -0.22, 0.18)
    return jnp.clip(drawn, -limit, limit).astype(dtype)


def setup_inputs(seed: int = 0, part: int = 0) -> dict:
    streams_of = jax.random.split(jax.random.key(seed), 7)
    own_keys = jax.random.split(jax.random.fold_in(streams_of[6], part), 7)
    return {
        "pair": normal_values(own_keys[0], (N, N, D), 1.0, 6.0, ((0, 16),)),
        "pair_mask": set_ends((jax.random.randint(own_keys[1], (N, N), 0, 4) < 3).astype(jnp.int32), jax.random.fold_in(own_keys[1], 1), 0, 1),
        "in_gain": jnp.clip(1.0 + 0.18 * jax.random.normal(streams_of[2], (D,), jnp.float32), 0.1, 1.9),
        "in_proj": normal_values(streams_of[3], (D, 4 * CH), D ** -0.5, 0.5),
        "gate_proj": normal_values(streams_of[4], (D, D), D ** -0.5, 0.5),
        "out_proj": normal_values(streams_of[5], (CH, D), CH ** -0.5, 0.5),
    }


def norm_last(values, eps):
    mean = lax.optimization_barrier(jnp.mean(values, axis=-1, keepdims=True))
    centered = values - mean
    variance = lax.optimization_barrier(jnp.mean(centered * centered, axis=-1, keepdims=True))
    return centered * jax.lax.rsqrt(variance + eps)

def reference(pair, pair_mask, in_gain, in_proj, gate_proj, out_proj):
    tokens = pair.shape[0]
    width = pair.shape[2]
    hidden = out_proj.shape[0]
    normed = (norm_last(pair.astype(jnp.float32), 1e-05) * in_gain).astype(jnp.bfloat16)
    flat = normed.reshape(tokens * tokens, width)
    proj = jnp.dot(flat, in_proj, preferred_element_type=jnp.float32).reshape(tokens, tokens, 4 * hidden)
    keep = pair_mask.astype(jnp.float32)[:, :, None]
    left = (keep * jax.nn.sigmoid(proj[:, :, hidden:2 * hidden]) * proj[:, :, :hidden]).astype(jnp.bfloat16)
    right = (keep * jax.nn.sigmoid(proj[:, :, 3 * hidden:]) * proj[:, :, 2 * hidden:3 * hidden]).astype(jnp.bfloat16)
    crossed = jnp.einsum('ikc,jkc->ijc', left.astype(jnp.float32), right.astype(jnp.float32)).astype(jnp.bfloat16)
    crossed_norm = norm_last(crossed.astype(jnp.float32), 1e-05).astype(jnp.bfloat16)
    gate = jax.nn.sigmoid(jnp.dot(flat, gate_proj, preferred_element_type=jnp.float32))
    mixed = jnp.dot(crossed_norm.reshape(tokens * tokens, hidden), out_proj, preferred_element_type=jnp.float32)
    return (gate * mixed).reshape(tokens, tokens, width).astype(jnp.bfloat16)
```

```python
import functools

import jax
import jax.numpy as jnp
from jax import lax
from jax.experimental import pallas as pl
from jax.experimental.pallas import tpu as pltpu
from jax.sharding import PartitionSpec as P

EPS = 1e-05
VMEM = pl.BlockSpec(memory_space=pltpu.VMEM)
SMEM = pl.BlockSpec(memory_space=pltpu.SMEM)
PARAMS = pltpu.CompilerParams(vmem_limit_bytes=48 * 2**20)
OVER_LAST = (((1,), (1,)), ((), ()))


def sigmoid(x):
    return 0.5 * jnp.tanh(0.5 * x) + 0.5


def normed_row(pair_ref, gain, r):
    x = pair_ref[r].astype(jnp.float32)
    centered = x - jnp.mean(x, axis=-1, keepdims=True)
    variance = jnp.mean(centered * centered, axis=-1, keepdims=True)
    return (centered * lax.rsqrt(variance + EPS) * gain).astype(jnp.bfloat16)


def operand(pair_ref, mask_ref, gain_ref, proj_ref, total, first):
    rows, tokens, _ = pair_ref.shape
    hidden = proj_ref.shape[1] // 4
    weights = proj_ref[:, first * hidden : (first + 2) * hidden].T
    gain = gain_ref[...]

    def step(r, carry):
        normed = normed_row(pair_ref, gain, r)
        proj = lax.dot_general(weights, normed, OVER_LAST, preferred_element_type=jnp.float32)
        keep = mask_ref[pl.ds(r, 1), :].astype(jnp.float32)
        value = keep * sigmoid(proj[hidden:]) * proj[:hidden]
        for t in range(tokens // 128):
            total[t, pl.ds(r, hidden, stride=rows), :] = value[:, t * 128 : (t + 1) * 128]
        return carry

    lax.fori_loop(0, rows, step, 0, unroll=4)


def right_kernel(pair_ref, mask_ref, gain_ref, proj_ref, out_ref, total):
    copies, blocks, group, rows, tokens = out_ref.shape
    operand(pair_ref, mask_ref, gain_ref, proj_ref, total, 2)
    for b in range(blocks):
        for t in range(tokens // 128):
            block = total[t, b * group * rows : (b + 1) * group * rows, :].astype(jnp.bfloat16)
            for c in range(copies):
                out_ref[c, b, :, :, t * 128 : (t + 1) * 128] = block.reshape(group, rows, 128)


def left_kernel(me_ref, pair_ref, mask_ref, gain_ref, proj_ref, *rest):
    *out_refs, total = rest
    blocks = len(out_refs)
    group, rows, tokens = out_refs[0].shape
    operand(pair_ref, mask_ref, gain_ref, proj_ref, total, 0)
    for s, out_ref in enumerate(out_refs):
        b = lax.rem(me_ref[0] + s, blocks)
        for t in range(tokens // 128):
            block = total[t, pl.ds(pl.multiple_of(b * group * rows, group * rows), group * rows), :]
            out_ref[:, :, t * 128 : (t + 1) * 128] = block.astype(jnp.bfloat16).reshape(group, rows, 128)


def cross_kernel(me_ref, right_ref, *rest):
    *left_refs, out_ref = rest
    blocks = len(left_refs)
    sources, group, rows, tokens = right_ref.shape
    for c in range(group):
        right = right_ref[:, c].reshape(sources * rows, tokens)
        left = jnp.concatenate([ref[c] for ref in left_refs], axis=0)
        crossed = lax.dot_general(left, right, OVER_LAST, preferred_element_type=jnp.float32)
        crossed = crossed.astype(jnp.bfloat16).reshape(blocks, rows, sources * rows)
        for s in range(blocks):
            owner = lax.rem(me_ref[0] + blocks - s, blocks)
            out_ref[owner, c] = crossed[s]


def gate_kernel(pair_ref, gain_ref, proj_ref, out_ref):
    rows = pair_ref.shape[0]
    gain = gain_ref[...]
    weights = proj_ref[...]

    def step(r, carry):
        normed = normed_row(pair_ref, gain, r)
        out_ref[r] = sigmoid(jnp.dot(normed, weights, preferred_element_type=jnp.float32))
        return carry

    lax.fori_loop(0, rows, step, 0, unroll=4)


def final_kernel(crossed_ref, gate_ref, proj_ref, out_ref, total):
    hidden, rows, tokens = crossed_ref.shape
    for t in range(tokens // 128):
        lanes = slice(t * 128, (t + 1) * 128)
        x = crossed_ref[:, :, lanes].astype(jnp.float32)
        centered = x - jnp.mean(x, axis=0, keepdims=True)
        variance = jnp.mean(centered * centered, axis=0, keepdims=True)
        total[t] = (centered * lax.rsqrt(variance + EPS)).reshape(hidden * rows, 128)
    weights = proj_ref[...]

    def step(r, carry):
        for t in range(tokens // 128):
            lanes = slice(t * 128, (t + 1) * 128)
            x = total[t, pl.ds(r, hidden, stride=rows), :].T.astype(jnp.bfloat16)
            mixed = jnp.dot(x, weights, preferred_element_type=jnp.float32)
            out_ref[r, lanes, :] = (gate_ref[r, lanes, :] * mixed).astype(jnp.bfloat16)
        return carry

    lax.fori_loop(0, rows, step, 0, unroll=4)


def call(kernel, out_shape, operands, scratch=(), cost=1.0):
    specs = [SMEM if x.dtype == jnp.int32 and x.ndim == 1 else VMEM for x in operands]
    return pl.pallas_call(
        kernel,
        out_shape=out_shape,
        in_specs=specs,
        out_specs=jax.tree.map(lambda _: VMEM, out_shape),
        scratch_shapes=list(scratch),
        compiler_params=PARAMS,
        cost_estimate=pl.CostEstimate(
            flops=int(cost * 1e9), bytes_accessed=int(cost * 4e6), transcendentals=0
        ),
    )(*operands)


def on_device(devices, pair, pair_mask, in_gain, in_proj, gate_proj, out_proj):
    rows, tokens, width = pair.shape
    hidden = out_proj.shape[0]
    blocks = devices // 2
    group = hidden // blocks
    sds = jax.ShapeDtypeStruct
    bf16 = jnp.bfloat16
    me = lax.rem(lax.axis_index("row"), blocks).astype(jnp.int32).reshape(1)
    gain = in_gain.reshape(1, width)
    total = pltpu.VMEM((tokens // 128, hidden * rows, 128), jnp.float32)

    right = call(
        right_kernel,
        sds((2, blocks, group, rows, tokens), bf16),
        (pair, pair_mask, gain, in_proj),
        (total,),
    ).reshape(devices, group, rows, tokens)
    right = lax.all_to_all(right, "row", split_axis=0, concat_axis=0, tiled=True)
    lefts = call(
        left_kernel,
        tuple(sds((group, rows, tokens), bf16) for _ in range(blocks)),
        (me, pair, pair_mask, gain, in_proj),
        (total,),
    )
    halves = (range(blocks), range(blocks, devices))
    lefts = [lefts[0]] + [
        lax.ppermute(
            lefts[s],
            "row",
            [(h[i], h[(i + s) % blocks]) for h in halves for i in range(blocks)],
        )
        for s in range(1, blocks)
    ]
    gate = call(gate_kernel, sds((rows, tokens, width), jnp.float32), (pair, gain, gate_proj))
    crossed = call(
        cross_kernel, sds((blocks, group, rows, devices * rows), bf16), (me, right, *lefts)
    )
    crossed = lax.all_to_all(
        crossed, "row", split_axis=0, concat_axis=0, tiled=True,
        axis_index_groups=[list(h) for h in halves],
    ).reshape(hidden, rows, tokens)
    return call(final_kernel, sds((rows, tokens, width), bf16), (crossed, gate, out_proj), (total,))


def solution(mesh):
    in_specs = (P(("parts", "row"), None, None), P(("parts", "row"), None), P(), P(), P(), P())
    out_specs = P(("parts", "row"), None, None)
    return jax.shard_map(
        functools.partial(on_device, mesh.shape["row"]),
        mesh=mesh, in_specs=in_specs, out_specs=out_specs, check_vma=False,
    )
```

```python
import functools

import jax
import jax.numpy as jnp
from jax import lax
from jax.experimental import pallas as pl
from jax.experimental.pallas import tpu as pltpu
from jax.sharding import PartitionSpec as P

EPS = 1e-05
VMEM = pl.BlockSpec(memory_space=pltpu.VMEM)
SMEM = pl.BlockSpec(memory_space=pltpu.SMEM)
ANY = pl.BlockSpec(memory_space=pl.ANY)
OVER_LAST = (((1,), (1,)), ((), ()))


def sigmoid(x):
    return 0.5 * jnp.tanh(0.5 * x) + 0.5


def normed_rows(pair, gain):
    x = pair.astype(jnp.float32)
    centered = x - jnp.mean(x, axis=-1, keepdims=True)
    variance = jnp.mean(centered * centered, axis=-1, keepdims=True)
    return (centered * lax.rsqrt(variance + EPS) * gain).astype(jnp.bfloat16)


def operand(pair_ref, mask_ref, gain_ref, proj_ref, total, first):
    rows, tokens, _ = pair_ref.shape
    hidden = proj_ref.shape[1] // 4
    weights = proj_ref[:, first * hidden : (first + 2) * hidden].T
    gain = gain_ref[...]

    def step(r, carry):
        normed = normed_rows(pair_ref[r], gain)
        proj = lax.dot_general(weights, normed, OVER_LAST, preferred_element_type=jnp.float32)
        keep = mask_ref[pl.ds(r, 1), :].astype(jnp.float32)
        value = keep * sigmoid(proj[hidden:]) * proj[:hidden]
        for t in range(tokens // 128):
            total[t, pl.ds(r, hidden, stride=rows), :] = value[:, t * 128 : (t + 1) * 128]
        return carry

    lax.fori_loop(0, rows, step, 0, unroll=4)


def right_kernel(
    pair_hbm, mask_hbm, gain_hbm, proj_hbm, out_hbm,
    pair_ref, mask_ref, gain_ref, weights_ref, total, staged, in_sems, out_sems,
):
    copies, blocks, group, rows, tokens = out_hbm.shape
    hidden = blocks * group
    loads = [
        pltpu.make_async_copy(source, target, in_sems.at[i])
        for i, (source, target) in enumerate((
            (pair_hbm, pair_ref),
            (proj_hbm.at[:, 2 * hidden : 4 * hidden], weights_ref),
            (mask_hbm, mask_ref),
            (gain_hbm, gain_ref),
        ))
    ]
    for load in loads:
        load.start()
    for load in loads:
        load.wait()
    weights = weights_ref[...].T
    gain = gain_ref[...]
    step = 4 if rows % 4 == 0 else 1
    for first in range(0, rows, step):
        x = pair_ref[first : first + step].reshape(step * tokens, -1)
        proj = lax.dot_general(
            weights, normed_rows(x, gain), OVER_LAST, preferred_element_type=jnp.float32
        )
        for r in range(first, first + step):
            of_row = proj[:, (r - first) * tokens : (r - first + 1) * tokens]
            keep = mask_ref[r : r + 1, :].astype(jnp.float32)
            value = keep * sigmoid(of_row[hidden:]) * of_row[:hidden]
            for t in range(tokens // 128):
                total[t, pl.ds(r, hidden, stride=rows), :] = value[:, t * 128 : (t + 1) * 128]
    stores = []
    for b in range(blocks):
        for t in range(tokens // 128):
            block = total[t, b * group * rows : (b + 1) * group * rows, :].astype(jnp.bfloat16)
            staged[b, :, :, t * 128 : (t + 1) * 128] = block.reshape(group, rows, 128)
        for c in range(copies):
            store = pltpu.make_async_copy(staged.at[b], out_hbm.at[c, b], out_sems.at[c, b])
            store.start()
            stores.append(store)
    for store in stores:
        store.wait()


def left_kernel(me_ref, pair_ref, mask_ref, gain_ref, proj_ref, *rest):
    *out_refs, total = rest
    blocks = len(out_refs)
    group, rows, tokens = out_refs[0].shape
    operand(pair_ref, mask_ref, gain_ref, proj_ref, total, 0)
    for s, out_ref in enumerate(out_refs):
        b = lax.rem(me_ref[0] + s, blocks)
        for t in range(tokens // 128):
            block = total[t, pl.ds(pl.multiple_of(b * group * rows, group * rows), group * rows), :]
            out_ref[:, :, t * 128 : (t + 1) * 128] = block.astype(jnp.bfloat16).reshape(group, rows, 128)


def cross_kernel(me_ref, right_ref, *rest):
    *left_refs, out_ref = rest
    blocks = len(left_refs)
    sources, group, rows, tokens = right_ref.shape
    for c in range(group):
        right = right_ref[:, c].reshape(sources * rows, tokens)
        left = jnp.concatenate([ref[c] for ref in left_refs], axis=0)
        crossed = lax.dot_general(left, right, OVER_LAST, preferred_element_type=jnp.float32)
        crossed = crossed.astype(jnp.bfloat16).reshape(blocks, rows, sources * rows)
        for s in range(blocks):
            owner = lax.rem(me_ref[0] + blocks - s, blocks)
            out_ref[owner, c] = crossed[s]


def gate_kernel(pair_ref, gain_ref, proj_ref, out_ref):
    rows = pair_ref.shape[0]
    gain = gain_ref[...]
    weights = proj_ref[...]

    def step(r, carry):
        normed = normed_rows(pair_ref[r], gain)
        out_ref[r] = sigmoid(jnp.dot(normed, weights, preferred_element_type=jnp.float32))
        return carry

    lax.fori_loop(0, rows, step, 0, unroll=4)


def final_kernel(crossed_ref, gate_ref, proj_ref, out_hbm, total, staged, sems):
    hidden, rows, tokens = crossed_ref.shape
    weights = proj_ref[...]
    stores = []
    for t in range(tokens // 128):
        lanes = slice(t * 128, (t + 1) * 128)
        x = crossed_ref[:, :, lanes].astype(jnp.float32)
        centered = x - jnp.mean(x, axis=0, keepdims=True)
        variance = jnp.mean(centered * centered, axis=0, keepdims=True)
        total[t] = (centered * lax.rsqrt(variance + EPS)).reshape(hidden * rows, 128)
        for r in range(rows):
            x = total[t, pl.ds(r, hidden, stride=rows), :].T.astype(jnp.bfloat16)
            mixed = jnp.dot(x, weights, preferred_element_type=jnp.float32)
            staged[r, lanes, :] = (gate_ref[r, lanes, :] * mixed).astype(jnp.bfloat16)
        part = pl.ds(t * 128, 128)
        store = pltpu.make_async_copy(staged.at[:, part], out_hbm.at[:, part], sems.at[t])
        store.start()
        stores.append(store)
    for store in stores:
        store.wait()


def call(kernel, out_shape, operands, scratch=(), cost=1.0, in_hbm=False, out_hbm=False):
    specs = [ANY for _ in operands] if in_hbm else [SMEM if x.dtype == jnp.int32 and x.ndim == 1 else VMEM for x in operands]
    return pl.pallas_call(
        kernel,
        out_shape=out_shape,
        in_specs=specs,
        out_specs=jax.tree.map(lambda _: ANY if out_hbm else VMEM, out_shape),
        scratch_shapes=list(scratch),
        compiler_params=pltpu.CompilerParams(vmem_limit_bytes=(62 if in_hbm else 48) * 2**20),
        cost_estimate=pl.CostEstimate(
            flops=int(cost * 1e9), bytes_accessed=int(cost * 4e6), transcendentals=0
        ),
    )(*operands)


def on_device(devices, pair, pair_mask, in_gain, in_proj, gate_proj, out_proj):
    rows, tokens, width = pair.shape
    hidden = out_proj.shape[0]
    blocks = devices // 2
    group = hidden // blocks
    sds = jax.ShapeDtypeStruct
    bf16 = jnp.bfloat16
    me = lax.rem(lax.axis_index("row"), blocks).astype(jnp.int32).reshape(1)
    gain = in_gain.reshape(1, width)
    total = pltpu.VMEM((tokens // 128, hidden * rows, 128), jnp.float32)

    right = call(
        right_kernel,
        sds((2, blocks, group, rows, tokens), bf16),
        (pair, pair_mask, gain, in_proj),
        (
            pltpu.VMEM(pair.shape, bf16),
            pltpu.VMEM(pair_mask.shape, jnp.int32),
            pltpu.VMEM(gain.shape, jnp.float32),
            pltpu.VMEM((width, 2 * hidden), bf16),
            total,
            pltpu.VMEM((blocks, group, rows, tokens), bf16),
            pltpu.SemaphoreType.DMA((4,)),
            pltpu.SemaphoreType.DMA((2, blocks)),
        ),
        in_hbm=True,
        out_hbm=True,
    ).reshape(devices, group, rows, tokens)
    right = lax.all_to_all(right, "row", split_axis=0, concat_axis=0, tiled=True)
    lefts = call(
        left_kernel,
        tuple(sds((group, rows, tokens), bf16) for _ in range(blocks)),
        (me, pair, pair_mask, gain, in_proj),
        (total,),
    )
    halves = (range(blocks), range(blocks, devices))
    lefts = [lefts[0]] + [
        lax.ppermute(
            lefts[s],
            "row",
            [(h[i], h[(i + s) % blocks]) for h in halves for i in range(blocks)],
        )
        for s in range(1, blocks)
    ]
    gate = call(gate_kernel, sds((rows, tokens, width), jnp.float32), (pair, gain, gate_proj))
    crossed = call(
        cross_kernel, sds((blocks, group, rows, devices * rows), bf16), (me, right, *lefts)
    )
    crossed = lax.all_to_all(
        crossed, "row", split_axis=0, concat_axis=0, tiled=True,
        axis_index_groups=[list(h) for h in halves],
    ).reshape(hidden, rows, tokens)
    return call(
        final_kernel,
        sds((rows, tokens, width), bf16),
        (crossed, gate, out_proj),
        (
            total,
            pltpu.VMEM((rows, tokens, width), bf16),
            pltpu.SemaphoreType.DMA((tokens // 128,)),
        ),
        out_hbm=True,
    )


def solution(mesh):
    in_specs = (P(("parts", "row"), None, None), P(("parts", "row"), None), P(), P(), P(), P())
    out_specs = P(("parts", "row"), None, None)
    return jax.shard_map(
        functools.partial(on_device, mesh.shape["row"]),
        mesh=mesh, in_specs=in_specs, out_specs=out_specs, check_vma=False,
    )
```

```python
import functools

import jax
import jax.numpy as jnp
from jax import lax
from jax.experimental import pallas as pl
from jax.experimental.pallas import tpu as pltpu
from jax.sharding import PartitionSpec as P

EPS = 1e-05
VMEM = pl.BlockSpec(memory_space=pltpu.VMEM)
SMEM = pl.BlockSpec(memory_space=pltpu.SMEM)
ANY = pl.BlockSpec(memory_space=pl.ANY)
OVER_LAST = (((1,), (1,)), ((), ()))


def steps_of(blocks):
    return (0, 1, 6, 2, 4, 7, 3, 5) if blocks == 8 else tuple(range(blocks))


def sigmoid(x):
    return 0.5 * jnp.tanh(0.5 * x) + 0.5


def normed_rows(pair, gain):
    x = pair.astype(jnp.float32)
    centered = x - jnp.mean(x, axis=-1, keepdims=True)
    variance = jnp.mean(centered * centered, axis=-1, keepdims=True)
    return (centered * lax.rsqrt(variance + EPS) * gain).astype(jnp.bfloat16)


def operand(pair_ref, mask_ref, gain_ref, proj_ref, total, first):
    rows, tokens, _ = pair_ref.shape
    hidden = proj_ref.shape[1] // 4
    weights = proj_ref[:, first * hidden : (first + 2) * hidden].T
    gain = gain_ref[...]

    def step(r, carry):
        normed = normed_rows(pair_ref[r], gain)
        proj = lax.dot_general(weights, normed, OVER_LAST, preferred_element_type=jnp.float32)
        keep = mask_ref[pl.ds(r, 1), :].astype(jnp.float32)
        value = keep * sigmoid(proj[hidden:]) * proj[:hidden]
        for t in range(tokens // 128):
            total[t, pl.ds(r, hidden, stride=rows), :] = value[:, t * 128 : (t + 1) * 128]
        return carry

    lax.fori_loop(0, rows, step, 0, unroll=4)


def right_kernel(
    pair_hbm, mask_hbm, gain_hbm, proj_hbm, out_hbm,
    pair_ref, mask_ref, gain_ref, weights_ref, total, staged, in_sems, out_sems,
):
    copies, blocks, group, rows, tokens = out_hbm.shape
    hidden = blocks * group
    loads = [
        pltpu.make_async_copy(source, target, in_sems.at[i])
        for i, (source, target) in enumerate((
            (pair_hbm, pair_ref),
            (proj_hbm.at[:, 2 * hidden : 4 * hidden], weights_ref),
            (mask_hbm, mask_ref),
            (gain_hbm, gain_ref),
        ))
    ]
    for load in loads:
        load.start()
    for load in loads:
        load.wait()
    weights = weights_ref[...].T
    gain = gain_ref[...]
    step = 4 if rows % 4 == 0 else 1
    for first in range(0, rows, step):
        x = pair_ref[first : first + step].reshape(step * tokens, -1)
        proj = lax.dot_general(
            weights, normed_rows(x, gain), OVER_LAST, preferred_element_type=jnp.float32
        )
        for r in range(first, first + step):
            of_row = proj[:, (r - first) * tokens : (r - first + 1) * tokens]
            keep = mask_ref[r : r + 1, :].astype(jnp.float32)
            value = keep * sigmoid(of_row[hidden:]) * of_row[:hidden]
            for t in range(tokens // 128):
                total[t, pl.ds(r, hidden, stride=rows), :] = value[:, t * 128 : (t + 1) * 128]
    stores = []
    for b in range(blocks):
        for t in range(tokens // 128):
            block = total[t, b * group * rows : (b + 1) * group * rows, :].astype(jnp.bfloat16)
            staged[b, :, :, t * 128 : (t + 1) * 128] = block.reshape(group, rows, 128)
        for c in range(copies):
            store = pltpu.make_async_copy(staged.at[b], out_hbm.at[c, b], out_sems.at[c, b])
            store.start()
            stores.append(store)
    for store in stores:
        store.wait()


def left_kernel(me_ref, pair_ref, mask_ref, gain_ref, proj_ref, *rest):
    *out_refs, total = rest
    blocks = len(out_refs)
    group, rows, tokens = out_refs[0].shape
    operand(pair_ref, mask_ref, gain_ref, proj_ref, total, 0)
    for step, out_ref in zip(steps_of(blocks), out_refs):
        b = me_ref[0] ^ step
        for t in range(tokens // 128):
            block = total[t, pl.ds(pl.multiple_of(b * group * rows, group * rows), group * rows), :]
            out_ref[:, :, t * 128 : (t + 1) * 128] = block.astype(jnp.bfloat16).reshape(group, rows, 128)


def cross_kernel(right_hbm, *rest):
    *refs, right_ref, sems = rest
    blocks = len(refs) // 2
    left_refs, out_refs = refs[:blocks], refs[blocks:]
    sources, group, rows, tokens = right_ref.shape
    parts = sems.shape[0]
    loads = []
    for part in range(parts):
        channels = pl.ds(part * (group // parts), group // parts)
        load = pltpu.make_async_copy(
            right_hbm.at[:, channels], right_ref.at[:, channels], sems.at[part]
        )
        load.start()
        loads.append(load)
    for c in range(group):
        if c % (group // parts) == 0:
            loads[c // (group // parts)].wait()
        right = right_ref[:, c].reshape(sources * rows, tokens)
        left = jnp.concatenate([ref[c] for ref in left_refs], axis=0)
        crossed = lax.dot_general(left, right, OVER_LAST, preferred_element_type=jnp.float32)
        crossed = crossed.astype(jnp.bfloat16).reshape(blocks, rows, sources * rows)
        for s, out_ref in enumerate(out_refs):
            out_ref[c] = crossed[s]


def gate_kernel(pair_ref, gain_ref, proj_ref, out_ref):
    rows = pair_ref.shape[0]
    gain = gain_ref[...]
    weights = proj_ref[...]

    def step(r, carry):
        normed = normed_rows(pair_ref[r], gain)
        out_ref[r] = sigmoid(jnp.dot(normed, weights, preferred_element_type=jnp.float32))
        return carry

    lax.fori_loop(0, rows, step, 0, unroll=4)


def final_kernel(me_ref, gate_ref, proj_ref, *rest):
    *crossed_refs, out_hbm, total, staged, sems = rest
    group, rows, tokens = crossed_refs[0].shape
    hidden = group * len(crossed_refs)
    weights = proj_ref[...]
    stores = []
    for t in range(tokens // 128):
        lanes = slice(t * 128, (t + 1) * 128)
        x = jnp.concatenate([ref[:, :, lanes] for ref in crossed_refs], axis=0)
        x = x.astype(jnp.float32)
        centered = x - jnp.mean(x, axis=0, keepdims=True)
        variance = jnp.mean(centered * centered, axis=0, keepdims=True)
        x = (centered * lax.rsqrt(variance + EPS)).reshape(len(crossed_refs), group * rows, 128)
        for s, step in enumerate(steps_of(len(crossed_refs))):
            owner = me_ref[0] ^ step
            first = pl.multiple_of(owner * (group * rows), group * rows)
            total[t, pl.ds(first, group * rows), :] = x[s]
        for r in range(rows):
            x = total[t, pl.ds(r, hidden, stride=rows), :].T.astype(jnp.bfloat16)
            mixed = jnp.dot(x, weights, preferred_element_type=jnp.float32)
            staged[r, lanes, :] = (gate_ref[r, lanes, :] * mixed).astype(jnp.bfloat16)
        part = pl.ds(t * 128, 128)
        store = pltpu.make_async_copy(staged.at[:, part], out_hbm.at[:, part], sems.at[t])
        store.start()
        stores.append(store)
    for store in stores:
        store.wait()


def call(kernel, out_shape, operands, scratch=(), in_hbm=(), out_hbm=False, limit=48, cost=1.0):
    specs = [
        ANY if i in in_hbm else SMEM if x.ndim == 1 else VMEM
        for i, x in enumerate(operands)
    ]
    return pl.pallas_call(
        kernel,
        out_shape=out_shape,
        in_specs=specs,
        out_specs=jax.tree.map(lambda _: ANY if out_hbm else VMEM, out_shape),
        scratch_shapes=list(scratch),
        compiler_params=pltpu.CompilerParams(vmem_limit_bytes=limit * 2**20),
        cost_estimate=pl.CostEstimate(
            flops=int(cost * 1e9), bytes_accessed=int(cost * 4e6), transcendentals=0
        ),
    )(*operands)


def exchange(parts, devices):
    return [
        lax.ppermute(part, "row", [(i, i ^ step) for i in range(devices)]) if step else part
        for part, step in zip(parts, steps_of(len(parts)))
    ]


def on_device(devices, pair, pair_mask, in_gain, in_proj, gate_proj, out_proj):
    rows, tokens, width = pair.shape
    hidden = out_proj.shape[0]
    blocks = devices // 2
    group = hidden // blocks
    sds = jax.ShapeDtypeStruct
    bf16 = jnp.bfloat16
    me = lax.rem(lax.axis_index("row"), blocks).astype(jnp.int32).reshape(1)
    gain = in_gain.reshape(1, width)
    total = pltpu.VMEM((tokens // 128, hidden * rows, 128), jnp.float32)

    right = call(
        right_kernel,
        sds((2, blocks, group, rows, tokens), bf16),
        (pair, pair_mask, gain, in_proj),
        (
            pltpu.VMEM(pair.shape, bf16),
            pltpu.VMEM(pair_mask.shape, jnp.int32),
            pltpu.VMEM(gain.shape, jnp.float32),
            pltpu.VMEM((width, 2 * hidden), bf16),
            total,
            pltpu.VMEM((blocks, group, rows, tokens), bf16),
            pltpu.SemaphoreType.DMA((4,)),
            pltpu.SemaphoreType.DMA((2, blocks)),
        ),
        in_hbm=range(4),
        out_hbm=True,
        limit=62,
    ).reshape(devices, group, rows, tokens)
    right = lax.all_to_all(right, "row", split_axis=0, concat_axis=0, tiled=True)
    right = pltpu.with_memory_space_constraint(right, pltpu.HBM)
    lefts = call(
        left_kernel,
        tuple(sds((group, rows, tokens), bf16) for _ in range(blocks)),
        (me, pair, pair_mask, gain, in_proj),
        (total,),
    )
    lefts = exchange(lefts, devices)
    gate = call(gate_kernel, sds((rows, tokens, width), jnp.float32), (pair, gain, gate_proj))
    crossed = call(
        cross_kernel,
        tuple(sds((group, rows, devices * rows), bf16) for _ in range(blocks)),
        (right, *lefts),
        (
            pltpu.VMEM(right.shape, bf16),
            pltpu.SemaphoreType.DMA((4 if group % 4 == 0 else 1,)),
        ),
        in_hbm=(0,),
    )
    crossed = exchange(crossed, devices)
    return call(
        final_kernel,
        sds((rows, tokens, width), bf16),
        (me, gate, out_proj, *crossed),
        (
            total,
            pltpu.VMEM((rows, tokens, width), bf16),
            pltpu.SemaphoreType.DMA((tokens // 128,)),
        ),
        out_hbm=True,
    )


def solution(mesh):
    in_specs = (P(("parts", "row"), None, None), P(("parts", "row"), None), P(), P(), P(), P())
    out_specs = P(("parts", "row"), None, None)
    return jax.shard_map(
        functools.partial(on_device, mesh.shape["row"]),
        mesh=mesh, in_specs=in_specs, out_specs=out_specs, check_vma=False,
    )
```

```python
import functools

import jax
import jax.numpy as jnp
from jax import lax
from jax.experimental import pallas as pl
from jax.experimental.pallas import tpu as pltpu
from jax.sharding import PartitionSpec as P

EPS = 1e-05
VMEM = pl.BlockSpec(memory_space=pltpu.VMEM)
SMEM = pl.BlockSpec(memory_space=pltpu.SMEM)
ANY = pl.BlockSpec(memory_space=pl.ANY)
OVER_LAST = (((1,), (1,)), ((), ()))


def steps_of(blocks):
    return (0, 1, 6, 2, 4, 7, 3, 5) if blocks == 8 else tuple(range(blocks))


def sigmoid(x):
    return 0.5 * jnp.tanh(0.5 * x) + 0.5


def normed_rows(pair, gain):
    x = pair.astype(jnp.float32)
    centered = x - jnp.mean(x, axis=-1, keepdims=True)
    variance = jnp.mean(centered * centered, axis=-1, keepdims=True)
    return (centered * lax.rsqrt(variance + EPS) * gain).astype(jnp.bfloat16)


def operand(pair_ref, mask_ref, gain_ref, proj_ref, total, first):
    rows, tokens, _ = pair_ref.shape
    hidden = proj_ref.shape[1] // 4
    weights = proj_ref[:, first * hidden : (first + 2) * hidden].T
    gain = gain_ref[...]

    def step(r, carry):
        normed = normed_rows(pair_ref[r], gain)
        proj = lax.dot_general(weights, normed, OVER_LAST, preferred_element_type=jnp.float32)
        keep = mask_ref[pl.ds(r, 1), :].astype(jnp.float32)
        value = keep * sigmoid(proj[hidden:]) * proj[:hidden]
        for t in range(tokens // 128):
            total[t, pl.ds(r, hidden, stride=rows), :] = value[:, t * 128 : (t + 1) * 128]
        return carry

    lax.fori_loop(0, rows, step, 0, unroll=4)


def right_kernel(
    pair_hbm, mask_hbm, gain_hbm, proj_hbm, out_hbm,
    pair_ref, mask_ref, gain_ref, weights_ref, total, staged, in_sems, out_sems,
):
    copies, blocks, group, rows, tokens = out_hbm.shape
    hidden = blocks * group
    loads = [
        pltpu.make_async_copy(source, target, in_sems.at[i])
        for i, (source, target) in enumerate((
            (pair_hbm, pair_ref),
            (proj_hbm.at[:, 2 * hidden : 4 * hidden], weights_ref),
            (mask_hbm, mask_ref),
            (gain_hbm, gain_ref),
        ))
    ]
    for load in loads:
        load.start()
    for load in loads:
        load.wait()
    weights = weights_ref[...].T
    gain = gain_ref[...]
    step = 4 if rows % 4 == 0 else 1
    for first in range(0, rows, step):
        x = pair_ref[first : first + step].reshape(step * tokens, -1)
        proj = lax.dot_general(
            weights, normed_rows(x, gain), OVER_LAST, preferred_element_type=jnp.float32
        )
        for r in range(first, first + step):
            of_row = proj[:, (r - first) * tokens : (r - first + 1) * tokens]
            keep = mask_ref[r : r + 1, :].astype(jnp.float32)
            value = keep * sigmoid(of_row[hidden:]) * of_row[:hidden]
            for t in range(tokens // 128):
                total[t, pl.ds(r, hidden, stride=rows), :] = value[:, t * 128 : (t + 1) * 128]
    stores = []
    for b in range(blocks):
        for t in range(tokens // 128):
            block = total[t, b * group * rows : (b + 1) * group * rows, :].astype(jnp.bfloat16)
            staged[b, :, :, t * 128 : (t + 1) * 128] = block.reshape(group, rows, 128)
        for c in range(copies):
            store = pltpu.make_async_copy(staged.at[b], out_hbm.at[c, b], out_sems.at[c, b])
            store.start()
            stores.append(store)
    for store in stores:
        store.wait()


def left_kernel(me_ref, pair_ref, mask_ref, gain_ref, proj_ref, *rest):
    *out_refs, total = rest
    blocks = len(out_refs)
    group, rows, tokens = out_refs[0].shape
    operand(pair_ref, mask_ref, gain_ref, proj_ref, total, 0)
    for step, out_ref in zip(steps_of(blocks), out_refs):
        b = me_ref[0] ^ step
        for t in range(tokens // 128):
            block = total[t, pl.ds(pl.multiple_of(b * group * rows, group * rows), group * rows), :]
            out_ref[:, :, t * 128 : (t + 1) * 128] = block.astype(jnp.bfloat16).reshape(group, rows, 128)


def cross_kernel(right_ref, *rest):
    blocks = len(rest) // 2
    left_refs, out_refs = rest[:blocks], rest[blocks:]
    sources, group, rows, tokens = right_ref.shape
    for c in range(group):
        right = right_ref[:, c].reshape(sources * rows, tokens)
        left = jnp.concatenate([ref[c] for ref in left_refs], axis=0)
        crossed = lax.dot_general(left, right, OVER_LAST, preferred_element_type=jnp.float32)
        crossed = crossed.astype(jnp.bfloat16).reshape(blocks, rows, sources * rows)
        for s, out_ref in enumerate(out_refs):
            out_ref[c] = crossed[s]


def gate_kernel(pair_hbm, gain_ref, proj_ref, out_ref, pair_ref, sem):
    load = pltpu.make_async_copy(pair_hbm, pair_ref, sem)
    load.start()
    rows = pair_ref.shape[0]
    gain = gain_ref[...]
    weights = proj_ref[...]
    load.wait()

    def step(r, carry):
        normed = normed_rows(pair_ref[r], gain)
        out_ref[r] = sigmoid(jnp.dot(normed, weights, preferred_element_type=jnp.float32))
        return carry

    lax.fori_loop(0, rows, step, 0, unroll=4)


def final_kernel(me_ref, gate_ref, proj_ref, *rest):
    *crossed_refs, out_hbm, total, staged, sems = rest
    group, rows, tokens = crossed_refs[0].shape
    hidden = group * len(crossed_refs)
    weights = proj_ref[...]
    stores = []
    for t in range(tokens // 128):
        lanes = slice(t * 128, (t + 1) * 128)
        x = jnp.concatenate([ref[:, :, lanes] for ref in crossed_refs], axis=0)
        x = x.astype(jnp.float32)
        centered = x - jnp.mean(x, axis=0, keepdims=True)
        variance = jnp.mean(centered * centered, axis=0, keepdims=True)
        x = (centered * lax.rsqrt(variance + EPS)).reshape(len(crossed_refs), group * rows, 128)
        for s, step in enumerate(steps_of(len(crossed_refs))):
            owner = me_ref[0] ^ step
            first = pl.multiple_of(owner * (group * rows), group * rows)
            total[t, pl.ds(first, group * rows), :] = x[s]
        for r in range(rows):
            x = total[t, pl.ds(r, hidden, stride=rows), :].T.astype(jnp.bfloat16)
            mixed = jnp.dot(x, weights, preferred_element_type=jnp.float32)
            staged[r, lanes, :] = (gate_ref[r, lanes, :] * mixed).astype(jnp.bfloat16)
        part = pl.ds(t * 128, 128)
        store = pltpu.make_async_copy(staged.at[:, part], out_hbm.at[:, part], sems.at[t])
        store.start()
        stores.append(store)
    for store in stores:
        store.wait()


def call(kernel, out_shape, operands, scratch=(), in_hbm=(), out_hbm=False, limit=48, cost=1.0):
    specs = [
        ANY if i in in_hbm else SMEM if x.ndim == 1 else VMEM
        for i, x in enumerate(operands)
    ]
    return pl.pallas_call(
        kernel,
        out_shape=out_shape,
        in_specs=specs,
        out_specs=jax.tree.map(lambda _: ANY if out_hbm else VMEM, out_shape),
        scratch_shapes=list(scratch),
        compiler_params=pltpu.CompilerParams(vmem_limit_bytes=limit * 2**20),
        cost_estimate=pl.CostEstimate(
            flops=int(cost * 1e9), bytes_accessed=int(cost * 4e6), transcendentals=0
        ),
    )(*operands)


def exchange(parts, devices):
    return [
        lax.ppermute(part, "row", [(i, i ^ step) for i in range(devices)]) if step else part
        for part, step in zip(parts, steps_of(len(parts)))
    ]


def on_device(devices, pair, pair_mask, in_gain, in_proj, gate_proj, out_proj):
    rows, tokens, width = pair.shape
    hidden = out_proj.shape[0]
    blocks = devices // 2
    group = hidden // blocks
    sds = jax.ShapeDtypeStruct
    bf16 = jnp.bfloat16
    me = lax.rem(lax.axis_index("row"), blocks).astype(jnp.int32).reshape(1)
    gain = in_gain.reshape(1, width)
    total = pltpu.VMEM((tokens // 128, hidden * rows, 128), jnp.float32)

    right = call(
        right_kernel,
        sds((2, blocks, group, rows, tokens), bf16),
        (pair, pair_mask, gain, in_proj),
        (
            pltpu.VMEM(pair.shape, bf16),
            pltpu.VMEM(pair_mask.shape, jnp.int32),
            pltpu.VMEM(gain.shape, jnp.float32),
            pltpu.VMEM((width, 2 * hidden), bf16),
            total,
            pltpu.VMEM((blocks, group, rows, tokens), bf16),
            pltpu.SemaphoreType.DMA((4,)),
            pltpu.SemaphoreType.DMA((2, blocks)),
        ),
        in_hbm=range(4),
        out_hbm=True,
        limit=62,
    ).reshape(devices, group, rows, tokens)
    right = lax.all_to_all(right, "row", split_axis=0, concat_axis=0, tiled=True)
    lefts = call(
        left_kernel,
        tuple(sds((group, rows, tokens), bf16) for _ in range(blocks)),
        (me, pair, pair_mask, gain, in_proj),
        (total,),
    )
    lefts = exchange(lefts, devices)
    gate = call(
        gate_kernel,
        sds((rows, tokens, width), jnp.float32),
        (pltpu.with_memory_space_constraint(pair, pltpu.HBM), gain, gate_proj),
        (pltpu.VMEM(pair.shape, bf16), pltpu.SemaphoreType.DMA),
        in_hbm=(0,),
    )
    crossed = call(
        cross_kernel,
        tuple(sds((group, rows, devices * rows), bf16) for _ in range(blocks)),
        (right, *lefts),
    )
    crossed = exchange(crossed, devices)
    return call(
        final_kernel,
        sds((rows, tokens, width), bf16),
        (me, gate, out_proj, *crossed),
        (
            total,
            pltpu.VMEM((rows, tokens, width), bf16),
            pltpu.SemaphoreType.DMA((tokens // 128,)),
        ),
        out_hbm=True,
    )


def solution(mesh):
    in_specs = (P(("parts", "row"), None, None), P(("parts", "row"), None), P(), P(), P(), P())
    out_specs = P(("parts", "row"), None, None)
    return jax.shard_map(
        functools.partial(on_device, mesh.shape["row"]),
        mesh=mesh, in_specs=in_specs, out_specs=out_specs, check_vma=False,
    )
```

```python
import functools

import jax
import jax.numpy as jnp
from jax import lax
from jax.experimental import pallas as pl
from jax.experimental.pallas import tpu as pltpu
from jax.sharding import PartitionSpec as P

EPS = 1e-05
VMEM = pl.BlockSpec(memory_space=pltpu.VMEM)
SMEM = pl.BlockSpec(memory_space=pltpu.SMEM)
ANY = pl.BlockSpec(memory_space=pl.ANY)
OVER_LAST = (((1,), (1,)), ((), ()))


def steps_of(blocks):
    return (0, 1, 6, 2, 4, 7, 3, 5) if blocks == 8 else tuple(range(blocks))


def sigmoid(x):
    return 0.5 * jnp.tanh(0.5 * x) + 0.5


def normed_rows(pair, gain):
    x = pair.astype(jnp.float32)
    centered = x - jnp.mean(x, axis=-1, keepdims=True)
    variance = jnp.mean(centered * centered, axis=-1, keepdims=True)
    return (centered * lax.rsqrt(variance + EPS) * gain).astype(jnp.bfloat16)


def operand(pair_ref, mask_ref, gain_ref, proj_ref, total, first):
    rows, tokens, _ = pair_ref.shape
    hidden = proj_ref.shape[1] // 4
    weights = proj_ref[:, first * hidden : (first + 2) * hidden].T
    gain = gain_ref[...]

    def step(r, carry):
        normed = normed_rows(pair_ref[r], gain)
        proj = lax.dot_general(weights, normed, OVER_LAST, preferred_element_type=jnp.float32)
        keep = mask_ref[pl.ds(r, 1), :].astype(jnp.float32)
        value = keep * sigmoid(proj[hidden:]) * proj[:hidden]
        for t in range(tokens // 128):
            total[t, pl.ds(r, hidden, stride=rows), :] = value[:, t * 128 : (t + 1) * 128]
        return carry

    lax.fori_loop(0, rows, step, 0, unroll=4)


def right_kernel(
    pair_hbm, mask_hbm, gain_hbm, proj_hbm, out_hbm,
    pair_ref, mask_ref, gain_ref, weights_ref, total, staged, in_sems, out_sems,
):
    copies, blocks, group, rows, tokens = out_hbm.shape
    hidden = blocks * group
    chunks = tokens // 128
    loads = [
        pltpu.make_async_copy(
            pair_hbm.at[:, pl.ds(t * 128, 128)], pair_ref.at[:, pl.ds(t * 128, 128)], in_sems.at[t]
        )
        for t in range(chunks)
    ]
    small_loads = [
        pltpu.make_async_copy(source, target, in_sems.at[chunks + i])
        for i, (source, target) in enumerate((
            (proj_hbm.at[:, 2 * hidden : 4 * hidden], weights_ref),
            (mask_hbm, mask_ref),
            (gain_hbm, gain_ref),
        ))
    ]
    for load in loads[:1] + small_loads + loads[1:]:
        load.start()
    for load in small_loads:
        load.wait()
    weights = weights_ref[...].T
    gain = gain_ref[...]
    stores = []
    for t in range(chunks):
        lanes = slice(t * 128, (t + 1) * 128)
        loads[t].wait()
        normed = normed_rows(pair_ref[:, lanes].reshape(rows * 128, -1), gain)
        proj = lax.dot_general(weights, normed, OVER_LAST, preferred_element_type=jnp.float32)
        for r in range(rows):
            of_row = proj[:, r * 128 : (r + 1) * 128]
            keep = mask_ref[r : r + 1, lanes].astype(jnp.float32)
            total[t, pl.ds(r, hidden, stride=rows), :] = (
                keep * sigmoid(of_row[hidden:]) * of_row[:hidden]
            )
        for b in range(blocks):
            block = total[t, b * group * rows : (b + 1) * group * rows, :].astype(jnp.bfloat16)
            staged[b, :, :, lanes] = block.reshape(group, rows, 128)
            part = pl.ds(t * 128, 128)
            for c in range(copies):
                store = pltpu.make_async_copy(
                    staged.at[b, :, :, part], out_hbm.at[c, b, :, :, part], out_sems.at[c, b, t]
                )
                store.start()
                stores.append(store)
    for store in stores:
        store.wait()


def left_kernel(me_ref, pair_ref, mask_ref, gain_ref, proj_ref, *rest):
    *out_refs, total = rest
    blocks = len(out_refs)
    group, rows, tokens = out_refs[0].shape
    operand(pair_ref, mask_ref, gain_ref, proj_ref, total, 0)
    for step, out_ref in zip(steps_of(blocks), out_refs):
        b = me_ref[0] ^ step
        for t in range(tokens // 128):
            block = total[t, pl.ds(pl.multiple_of(b * group * rows, group * rows), group * rows), :]
            out_ref[:, :, t * 128 : (t + 1) * 128] = block.astype(jnp.bfloat16).reshape(group, rows, 128)


def cross_kernel(right_ref, *rest):
    blocks = len(rest) // 2
    left_refs, out_refs = rest[:blocks], rest[blocks:]
    sources, group, rows, tokens = right_ref.shape
    for c in range(group):
        right = right_ref[:, c].reshape(sources * rows, tokens)
        left = jnp.concatenate([ref[c] for ref in left_refs], axis=0)
        crossed = lax.dot_general(left, right, OVER_LAST, preferred_element_type=jnp.float32)
        crossed = crossed.astype(jnp.bfloat16).reshape(blocks, rows, sources * rows)
        for s, out_ref in enumerate(out_refs):
            out_ref[c] = crossed[s]


def gate_kernel(pair_hbm, gain_ref, proj_ref, out_ref, pair_ref, sem):
    load = pltpu.make_async_copy(pair_hbm, pair_ref, sem)
    load.start()
    rows = pair_ref.shape[0]
    gain = gain_ref[...]
    weights = proj_ref[...]
    load.wait()

    def step(r, carry):
        normed = normed_rows(pair_ref[r], gain)
        out_ref[r] = sigmoid(jnp.dot(normed, weights, preferred_element_type=jnp.float32))
        return carry

    lax.fori_loop(0, rows, step, 0, unroll=4)


def final_kernel(me_ref, gate_ref, proj_ref, *rest):
    *crossed_refs, out_hbm, total, staged, sems = rest
    group, rows, tokens = crossed_refs[0].shape
    hidden = group * len(crossed_refs)
    weights = proj_ref[...]
    stores = []
    for t in range(tokens // 128):
        lanes = slice(t * 128, (t + 1) * 128)
        x = jnp.concatenate([ref[:, :, lanes] for ref in crossed_refs], axis=0)
        x = x.astype(jnp.float32)
        centered = x - jnp.mean(x, axis=0, keepdims=True)
        variance = jnp.mean(centered * centered, axis=0, keepdims=True)
        x = (centered * lax.rsqrt(variance + EPS)).reshape(len(crossed_refs), group * rows, 128)
        for s, step in enumerate(steps_of(len(crossed_refs))):
            owner = me_ref[0] ^ step
            first = pl.multiple_of(owner * (group * rows), group * rows)
            total[t, pl.ds(first, group * rows), :] = x[s]
        for r in range(rows):
            x = total[t, pl.ds(r, hidden, stride=rows), :].T.astype(jnp.bfloat16)
            mixed = jnp.dot(x, weights, preferred_element_type=jnp.float32)
            staged[r, lanes, :] = (gate_ref[r, lanes, :] * mixed).astype(jnp.bfloat16)
        part = pl.ds(t * 128, 128)
        store = pltpu.make_async_copy(staged.at[:, part], out_hbm.at[:, part], sems.at[t])
        store.start()
        stores.append(store)
    for store in stores:
        store.wait()


def call(kernel, out_shape, operands, scratch=(), in_hbm=(), out_hbm=False, limit=48, cost=1.0):
    specs = [
        ANY if i in in_hbm else SMEM if x.ndim == 1 else VMEM
        for i, x in enumerate(operands)
    ]
    return pl.pallas_call(
        kernel,
        out_shape=out_shape,
        in_specs=specs,
        out_specs=jax.tree.map(lambda _: ANY if out_hbm else VMEM, out_shape),
        scratch_shapes=list(scratch),
        compiler_params=pltpu.CompilerParams(vmem_limit_bytes=limit * 2**20),
        cost_estimate=pl.CostEstimate(
            flops=int(cost * 1e9), bytes_accessed=int(cost * 4e6), transcendentals=0
        ),
    )(*operands)


def exchange(parts, devices):
    return [
        lax.ppermute(part, "row", [(i, i ^ step) for i in range(devices)]) if step else part
        for part, step in zip(parts, steps_of(len(parts)))
    ]


def on_device(devices, pair, pair_mask, in_gain, in_proj, gate_proj, out_proj):
    rows, tokens, width = pair.shape
    hidden = out_proj.shape[0]
    blocks = devices // 2
    group = hidden // blocks
    sds = jax.ShapeDtypeStruct
    bf16 = jnp.bfloat16
    me = lax.rem(lax.axis_index("row"), blocks).astype(jnp.int32).reshape(1)
    gain = in_gain.reshape(1, width)
    total = pltpu.VMEM((tokens // 128, hidden * rows, 128), jnp.float32)

    right = call(
        right_kernel,
        sds((2, blocks, group, rows, tokens), bf16),
        (pair, pair_mask, gain, in_proj),
        (
            pltpu.VMEM(pair.shape, bf16),
            pltpu.VMEM(pair_mask.shape, jnp.int32),
            pltpu.VMEM(gain.shape, jnp.float32),
            pltpu.VMEM((width, 2 * hidden), bf16),
            total,
            pltpu.VMEM((blocks, group, rows, tokens), bf16),
            pltpu.SemaphoreType.DMA((tokens // 128 + 3,)),
            pltpu.SemaphoreType.DMA((2, blocks, tokens // 128)),
        ),
        in_hbm=range(4),
        out_hbm=True,
        limit=62,
    ).reshape(devices, group, rows, tokens)
    right = lax.all_to_all(right, "row", split_axis=0, concat_axis=0, tiled=True)
    lefts = call(
        left_kernel,
        tuple(sds((group, rows, tokens), bf16) for _ in range(blocks)),
        (me, pair, pair_mask, gain, in_proj),
        (total,),
    )
    lefts = exchange(lefts, devices)
    gate = call(
        gate_kernel,
        sds((rows, tokens, width), jnp.float32),
        (pltpu.with_memory_space_constraint(pair, pltpu.HBM), gain, gate_proj),
        (pltpu.VMEM(pair.shape, bf16), pltpu.SemaphoreType.DMA),
        in_hbm=(0,),
    )
    crossed = call(
        cross_kernel,
        tuple(sds((group, rows, devices * rows), bf16) for _ in range(blocks)),
        (right, *lefts),
    )
    crossed = exchange(crossed, devices)
    return call(
        final_kernel,
        sds((rows, tokens, width), bf16),
        (me, gate, out_proj, *crossed),
        (
            total,
            pltpu.VMEM((rows, tokens, width), bf16),
            pltpu.SemaphoreType.DMA((tokens // 128,)),
        ),
        out_hbm=True,
    )


def solution(mesh):
    in_specs = (P(("parts", "row"), None, None), P(("parts", "row"), None), P(), P(), P(), P())
    out_specs = P(("parts", "row"), None, None)
    return jax.shard_map(
        functools.partial(on_device, mesh.shape["row"]),
        mesh=mesh, in_specs=in_specs, out_specs=out_specs, check_vma=False,
    )
```

```python
import functools

import jax
import jax.numpy as jnp
from jax import lax
from jax.experimental import pallas as pl
from jax.experimental.pallas import tpu as pltpu
from jax.sharding import PartitionSpec as P

EPS = 1e-05
VMEM = pl.BlockSpec(memory_space=pltpu.VMEM)
SMEM = pl.BlockSpec(memory_space=pltpu.SMEM)
ANY = pl.BlockSpec(memory_space=pl.ANY)
OVER_LAST = (((1,), (1,)), ((), ()))


def steps_of(blocks):
    return (0, 1, 6, 2, 4, 7, 3, 5) if blocks == 8 else tuple(range(blocks))


def sigmoid(x):
    return 0.5 * jnp.tanh(0.5 * x) + 0.5


def normed_rows(pair, gain):
    x = pair.astype(jnp.float32)
    centered = x - jnp.mean(x, axis=-1, keepdims=True)
    variance = jnp.mean(centered * centered, axis=-1, keepdims=True)
    return (centered * lax.rsqrt(variance + EPS) * gain).astype(jnp.bfloat16)


def gated(pair_ref, mask_ref, weights, gain, total, t):
    rows = pair_ref.shape[0]
    hidden = weights.shape[0] // 2
    lanes = slice(t * 128, (t + 1) * 128)
    normed = normed_rows(pair_ref[:, lanes].reshape(rows * 128, -1), gain)
    proj = lax.dot_general(weights, normed, OVER_LAST, preferred_element_type=jnp.float32)
    for r in range(rows):
        of_row = proj[:, r * 128 : (r + 1) * 128]
        keep = mask_ref[r : r + 1, lanes].astype(jnp.float32)
        total[t, pl.ds(r, hidden, stride=rows), :] = (
            keep * sigmoid(of_row[hidden:]) * of_row[:hidden]
        )


def right_kernel(
    pair_hbm, mask_hbm, gain_hbm, proj_hbm, out_hbm,
    pair_ref, mask_ref, gain_ref, weights_ref, total, staged, in_sems, out_sems,
):
    copies, blocks, group, rows, tokens = out_hbm.shape
    hidden = blocks * group
    chunks = tokens // 128
    loads = [
        pltpu.make_async_copy(
            pair_hbm.at[:, pl.ds(t * 128, 128)], pair_ref.at[:, pl.ds(t * 128, 128)], in_sems.at[t]
        )
        for t in range(chunks)
    ]
    small_loads = [
        pltpu.make_async_copy(source, target, in_sems.at[chunks + i])
        for i, (source, target) in enumerate((
            (proj_hbm.at[:, 2 * hidden : 4 * hidden], weights_ref),
            (mask_hbm, mask_ref),
            (gain_hbm, gain_ref),
        ))
    ]
    for load in loads[:1] + small_loads + loads[1:]:
        load.start()
    for load in small_loads:
        load.wait()
    weights = weights_ref[...].T
    gain = gain_ref[...]
    stores = []
    for t in range(chunks):
        lanes = slice(t * 128, (t + 1) * 128)
        loads[t].wait()
        gated(pair_ref, mask_ref, weights, gain, total, t)
        for b in range(blocks):
            block = total[t, b * group * rows : (b + 1) * group * rows, :].astype(jnp.bfloat16)
            staged[b, :, :, lanes] = block.reshape(group, rows, 128)
            part = pl.ds(t * 128, 128)
            for c in range(copies):
                store = pltpu.make_async_copy(
                    staged.at[b, :, :, part], out_hbm.at[c, b, :, :, part], out_sems.at[c, b, t]
                )
                store.start()
                stores.append(store)
    for store in stores:
        store.wait()


def left_kernel(me_ref, pair_ref, mask_ref, gain_ref, proj_ref, *rest):
    *out_refs, total = rest
    blocks = len(out_refs)
    group, rows, tokens = out_refs[0].shape
    weights = proj_ref[:, : 2 * blocks * group].T
    gain = gain_ref[...]
    for t in range(tokens // 128):
        gated(pair_ref, mask_ref, weights, gain, total, t)
        for step, out_ref in zip(steps_of(blocks), out_refs):
            first = pl.multiple_of((me_ref[0] ^ step) * (group * rows), group * rows)
            block = total[t, pl.ds(first, group * rows), :].astype(jnp.bfloat16)
            out_ref[:, :, t * 128 : (t + 1) * 128] = block.reshape(group, rows, 128)


def cross_kernel(right_ref, *rest):
    blocks = len(rest) // 2
    left_refs, out_refs = rest[:blocks], rest[blocks:]
    sources, group, rows, tokens = right_ref.shape
    for c in range(group):
        right = right_ref[:, c].reshape(sources * rows, tokens)
        left = jnp.concatenate([ref[c] for ref in left_refs], axis=0)
        crossed = lax.dot_general(left, right, OVER_LAST, preferred_element_type=jnp.float32)
        crossed = crossed.astype(jnp.bfloat16).reshape(blocks, rows, sources * rows)
        for s, out_ref in enumerate(out_refs):
            out_ref[c] = crossed[s]


def gate_kernel(pair_hbm, gain_ref, proj_ref, out_ref, pair_ref, sem):
    load = pltpu.make_async_copy(pair_hbm, pair_ref, sem)
    load.start()
    rows = pair_ref.shape[0]
    gain = gain_ref[...]
    weights = proj_ref[...]
    load.wait()

    def step(r, carry):
        normed = normed_rows(pair_ref[r], gain)
        out_ref[r] = sigmoid(jnp.dot(normed, weights, preferred_element_type=jnp.float32))
        return carry

    lax.fori_loop(0, rows, step, 0, unroll=4)


def final_kernel(me_ref, gate_ref, proj_ref, *rest):
    *crossed_refs, out_hbm, total, staged, sems = rest
    group, rows, tokens = crossed_refs[0].shape
    hidden = group * len(crossed_refs)
    weights = proj_ref[...]
    stores = []
    for t in range(tokens // 128):
        lanes = slice(t * 128, (t + 1) * 128)
        x = jnp.concatenate([ref[:, :, lanes] for ref in crossed_refs], axis=0)
        x = x.astype(jnp.float32)
        centered = x - jnp.mean(x, axis=0, keepdims=True)
        variance = jnp.mean(centered * centered, axis=0, keepdims=True)
        x = (centered * lax.rsqrt(variance + EPS)).reshape(len(crossed_refs), group * rows, 128)
        for s, step in enumerate(steps_of(len(crossed_refs))):
            owner = me_ref[0] ^ step
            first = pl.multiple_of(owner * (group * rows), group * rows)
            total[t, pl.ds(first, group * rows), :] = x[s]
        for r in range(rows):
            x = total[t, pl.ds(r, hidden, stride=rows), :].T.astype(jnp.bfloat16)
            mixed = jnp.dot(x, weights, preferred_element_type=jnp.float32)
            staged[r, lanes, :] = (gate_ref[r, lanes, :] * mixed).astype(jnp.bfloat16)
        part = pl.ds(t * 128, 128)
        store = pltpu.make_async_copy(staged.at[:, part], out_hbm.at[:, part], sems.at[t])
        store.start()
        stores.append(store)
    for store in stores:
        store.wait()


def call(kernel, out_shape, operands, scratch=(), in_hbm=(), out_hbm=False, limit=48, cost=1.0):
    specs = [
        ANY if i in in_hbm else SMEM if x.ndim == 1 else VMEM
        for i, x in enumerate(operands)
    ]
    return pl.pallas_call(
        kernel,
        out_shape=out_shape,
        in_specs=specs,
        out_specs=jax.tree.map(lambda _: ANY if out_hbm else VMEM, out_shape),
        scratch_shapes=list(scratch),
        compiler_params=pltpu.CompilerParams(vmem_limit_bytes=limit * 2**20),
        cost_estimate=pl.CostEstimate(
            flops=int(cost * 1e9), bytes_accessed=int(cost * 4e6), transcendentals=0
        ),
    )(*operands)


def exchange(parts, devices):
    return [
        lax.ppermute(part, "row", [(i, i ^ step) for i in range(devices)]) if step else part
        for part, step in zip(parts, steps_of(len(parts)))
    ]


def on_device(devices, pair, pair_mask, in_gain, in_proj, gate_proj, out_proj):
    rows, tokens, width = pair.shape
    hidden = out_proj.shape[0]
    blocks = devices // 2
    group = hidden // blocks
    sds = jax.ShapeDtypeStruct
    bf16 = jnp.bfloat16
    me = lax.rem(lax.axis_index("row"), blocks).astype(jnp.int32).reshape(1)
    gain = in_gain.reshape(1, width)
    total = pltpu.VMEM((tokens // 128, (hidden + 1) * rows, 128), jnp.float32)

    right = call(
        right_kernel,
        sds((2, blocks, group, rows, tokens), bf16),
        (pair, pair_mask, gain, in_proj),
        (
            pltpu.VMEM(pair.shape, bf16),
            pltpu.VMEM(pair_mask.shape, jnp.int32),
            pltpu.VMEM(gain.shape, jnp.float32),
            pltpu.VMEM((width, 2 * hidden), bf16),
            total,
            pltpu.VMEM((blocks, group, rows, tokens), bf16),
            pltpu.SemaphoreType.DMA((tokens // 128 + 3,)),
            pltpu.SemaphoreType.DMA((2, blocks, tokens // 128)),
        ),
        in_hbm=range(4),
        out_hbm=True,
        limit=62,
    ).reshape(devices, group, rows, tokens)
    right = lax.all_to_all(right, "row", split_axis=0, concat_axis=0, tiled=True)
    lefts = call(
        left_kernel,
        tuple(sds((group, rows, tokens), bf16) for _ in range(blocks)),
        (me, pair, pair_mask, gain, in_proj),
        (total,),
    )
    lefts = exchange(lefts, devices)
    gate = call(
        gate_kernel,
        sds((rows, tokens, width), jnp.float32),
        (pltpu.with_memory_space_constraint(pair, pltpu.HBM), gain, gate_proj),
        (pltpu.VMEM(pair.shape, bf16), pltpu.SemaphoreType.DMA),
        in_hbm=(0,),
    )
    crossed = call(
        cross_kernel,
        tuple(sds((group, rows, devices * rows), bf16) for _ in range(blocks)),
        (right, *lefts),
    )
    crossed = exchange(crossed, devices)
    return call(
        final_kernel,
        sds((rows, tokens, width), bf16),
        (me, gate, out_proj, *crossed),
        (
            total,
            pltpu.VMEM((rows, tokens, width), bf16),
            pltpu.SemaphoreType.DMA((tokens // 128,)),
        ),
        out_hbm=True,
    )


def solution(mesh):
    in_specs = (P(("parts", "row"), None, None), P(("parts", "row"), None), P(), P(), P(), P())
    out_specs = P(("parts", "row"), None, None)
    return jax.shard_map(
        functools.partial(on_device, mesh.shape["row"]),
        mesh=mesh, in_specs=in_specs, out_specs=out_specs, check_vma=False,
    )
```

```python
import functools

import jax
import jax.numpy as jnp
from jax import lax
from jax.experimental import pallas as pl
from jax.experimental.pallas import tpu as pltpu
from jax.sharding import PartitionSpec as P

EPS = 1e-05
VMEM = pl.BlockSpec(memory_space=pltpu.VMEM)
SMEM = pl.BlockSpec(memory_space=pltpu.SMEM)
ANY = pl.BlockSpec(memory_space=pl.ANY)
OVER_LAST = (((1,), (1,)), ((), ()))


def steps_of(blocks):
    return (0, 1, 6, 2, 4, 7, 3, 5) if blocks == 8 else tuple(range(blocks))


def sigmoid(x):
    return 0.5 * jnp.tanh(0.5 * x) + 0.5


def normed_rows(pair, gain, mean_by_dot=False):
    x = pair.astype(jnp.float32)
    if mean_by_dot:
        width = pair.shape[1]
        ones = jnp.full((width, width), 1 / width, jnp.bfloat16)
        mean = jnp.dot(pair, ones, preferred_element_type=jnp.float32)
    else:
        mean = jnp.mean(x, axis=-1, keepdims=True)
    centered = x - mean
    variance = jnp.mean(centered * centered, axis=-1, keepdims=True)
    return (centered * lax.rsqrt(variance + EPS) * gain).astype(jnp.bfloat16)


def gated(pair_ref, mask_ref, weights, gain, total, t):
    rows = pair_ref.shape[0]
    hidden = weights.shape[0] // 2
    lanes = slice(t * 128, (t + 1) * 128)
    normed = normed_rows(pair_ref[:, lanes].reshape(rows * 128, -1), gain, mean_by_dot=True)
    proj = lax.dot_general(weights, normed, OVER_LAST, preferred_element_type=jnp.float32)
    for r in range(rows):
        of_row = proj[:, r * 128 : (r + 1) * 128]
        keep = mask_ref[r : r + 1, lanes].astype(jnp.float32)
        total[t, pl.ds(r, hidden, stride=rows), :] = (
            keep * sigmoid(of_row[hidden:]) * of_row[:hidden]
        )


def right_kernel(
    pair_hbm, mask_hbm, gain_hbm, proj_hbm, out_hbm,
    pair_ref, mask_ref, gain_ref, weights_ref, total, staged, in_sems, out_sems,
):
    copies, blocks, group, rows, tokens = out_hbm.shape
    hidden = blocks * group
    chunks = tokens // 128
    loads = [
        pltpu.make_async_copy(
            pair_hbm.at[:, pl.ds(t * 128, 128)], pair_ref.at[:, pl.ds(t * 128, 128)], in_sems.at[t]
        )
        for t in range(chunks)
    ]
    small_loads = [
        pltpu.make_async_copy(source, target, in_sems.at[chunks + i])
        for i, (source, target) in enumerate((
            (proj_hbm.at[:, 2 * hidden : 4 * hidden], weights_ref),
            (mask_hbm, mask_ref),
            (gain_hbm, gain_ref),
        ))
    ]
    for load in loads[:1] + small_loads + loads[1:]:
        load.start()
    for load in small_loads:
        load.wait()
    weights = weights_ref[...].T
    gain = gain_ref[...]
    stores = []
    for t in range(chunks):
        lanes = slice(t * 128, (t + 1) * 128)
        loads[t].wait()
        gated(pair_ref, mask_ref, weights, gain, total, t)
        for b in range(blocks):
            block = total[t, b * group * rows : (b + 1) * group * rows, :].astype(jnp.bfloat16)
            staged[b, :, :, lanes] = block.reshape(group, rows, 128)
            part = pl.ds(t * 128, 128)
            for c in range(copies):
                store = pltpu.make_async_copy(
                    staged.at[b, :, :, part], out_hbm.at[c, b, :, :, part], out_sems.at[c, b, t]
                )
                store.start()
                stores.append(store)
    for store in stores:
        store.wait()


def left_kernel(me_ref, pair_ref, mask_ref, gain_ref, proj_ref, *rest):
    *out_refs, total = rest
    blocks = len(out_refs)
    group, rows, tokens = out_refs[0].shape
    weights = proj_ref[:, : 2 * blocks * group].T
    gain = gain_ref[...]
    for t in range(tokens // 128):
        gated(pair_ref, mask_ref, weights, gain, total, t)
        for step, out_ref in zip(steps_of(blocks), out_refs):
            first = pl.multiple_of((me_ref[0] ^ step) * (group * rows), group * rows)
            block = total[t, pl.ds(first, group * rows), :].astype(jnp.bfloat16)
            out_ref[:, :, t * 128 : (t + 1) * 128] = block.reshape(group, rows, 128)


def cross_kernel(right_ref, *rest):
    blocks = len(rest) // 2
    left_refs, out_refs = rest[:blocks], rest[blocks:]
    sources, group, rows, tokens = right_ref.shape
    for c in range(group):
        right = right_ref[:, c].reshape(sources * rows, tokens)
        left = jnp.concatenate([ref[c] for ref in left_refs], axis=0)
        crossed = lax.dot_general(left, right, OVER_LAST, preferred_element_type=jnp.float32)
        crossed = crossed.astype(jnp.bfloat16).reshape(blocks, rows, sources * rows)
        for s, out_ref in enumerate(out_refs):
            out_ref[c] = crossed[s]


def gate_kernel(pair_hbm, gain_ref, proj_ref, out_ref, pair_ref, sem):
    load = pltpu.make_async_copy(pair_hbm, pair_ref, sem)
    load.start()
    rows = pair_ref.shape[0]
    gain = gain_ref[...]
    weights = proj_ref[...]
    load.wait()

    def step(r, carry):
        normed = normed_rows(pair_ref[r], gain)
        out_ref[r] = sigmoid(jnp.dot(normed, weights, preferred_element_type=jnp.float32))
        return carry

    lax.fori_loop(0, rows, step, 0, unroll=4)


def final_kernel(me_ref, gate_ref, proj_ref, *rest):
    *crossed_refs, out_hbm, total, staged, sems = rest
    group, rows, tokens = crossed_refs[0].shape
    hidden = group * len(crossed_refs)
    weights = proj_ref[...]
    stores = []
    for t in range(tokens // 128):
        lanes = slice(t * 128, (t + 1) * 128)
        x = jnp.concatenate([ref[:, :, lanes] for ref in crossed_refs], axis=0)
        x = x.astype(jnp.float32)
        centered = x - jnp.mean(x, axis=0, keepdims=True)
        variance = jnp.mean(centered * centered, axis=0, keepdims=True)
        x = (centered * lax.rsqrt(variance + EPS)).reshape(len(crossed_refs), group * rows, 128)
        for s, step in enumerate(steps_of(len(crossed_refs))):
            owner = me_ref[0] ^ step
            first = pl.multiple_of(owner * (group * rows), group * rows)
            total[t, pl.ds(first, group * rows), :] = x[s]
        for r in range(rows):
            x = total[t, pl.ds(r, hidden, stride=rows), :].T.astype(jnp.bfloat16)
            mixed = jnp.dot(x, weights, preferred_element_type=jnp.float32)
            staged[r, lanes, :] = (gate_ref[r, lanes, :] * mixed).astype(jnp.bfloat16)
        part = pl.ds(t * 128, 128)
        store = pltpu.make_async_copy(staged.at[:, part], out_hbm.at[:, part], sems.at[t])
        store.start()
        stores.append(store)
    for store in stores:
        store.wait()


def call(kernel, out_shape, operands, scratch=(), in_hbm=(), out_hbm=False, limit=48, cost=1.0):
    specs = [
        ANY if i in in_hbm else SMEM if x.ndim == 1 else VMEM
        for i, x in enumerate(operands)
    ]
    return pl.pallas_call(
        kernel,
        out_shape=out_shape,
        in_specs=specs,
        out_specs=jax.tree.map(lambda _: ANY if out_hbm else VMEM, out_shape),
        scratch_shapes=list(scratch),
        compiler_params=pltpu.CompilerParams(vmem_limit_bytes=limit * 2**20),
        cost_estimate=pl.CostEstimate(
            flops=int(cost * 1e9), bytes_accessed=int(cost * 4e6), transcendentals=0
        ),
    )(*operands)


def exchange(parts, devices):
    return [
        lax.ppermute(part, "row", [(i, i ^ step) for i in range(devices)]) if step else part
        for part, step in zip(parts, steps_of(len(parts)))
    ]


def on_device(devices, pair, pair_mask, in_gain, in_proj, gate_proj, out_proj):
    rows, tokens, width = pair.shape
    hidden = out_proj.shape[0]
    blocks = devices // 2
    group = hidden // blocks
    sds = jax.ShapeDtypeStruct
    bf16 = jnp.bfloat16
    me = lax.rem(lax.axis_index("row"), blocks).astype(jnp.int32).reshape(1)
    gain = in_gain.reshape(1, width)
    total = pltpu.VMEM((tokens // 128, (hidden + 1) * rows, 128), jnp.float32)

    right = call(
        right_kernel,
        sds((2, blocks, group, rows, tokens), bf16),
        (pair, pair_mask, gain, in_proj),
        (
            pltpu.VMEM(pair.shape, bf16),
            pltpu.VMEM(pair_mask.shape, jnp.int32),
            pltpu.VMEM(gain.shape, jnp.float32),
            pltpu.VMEM((width, 2 * hidden), bf16),
            total,
            pltpu.VMEM((blocks, group, rows, tokens), bf16),
            pltpu.SemaphoreType.DMA((tokens // 128 + 3,)),
            pltpu.SemaphoreType.DMA((2, blocks, tokens // 128)),
        ),
        in_hbm=range(4),
        out_hbm=True,
        limit=62,
    ).reshape(devices, group, rows, tokens)
    right = lax.all_to_all(right, "row", split_axis=0, concat_axis=0, tiled=True)
    lefts = call(
        left_kernel,
        tuple(sds((group, rows, tokens), bf16) for _ in range(blocks)),
        (me, pair, pair_mask, gain, in_proj),
        (total,),
    )
    lefts = exchange(lefts, devices)
    gate = call(
        gate_kernel,
        sds((rows, tokens, width), jnp.float32),
        (pltpu.with_memory_space_constraint(pair, pltpu.HBM), gain, gate_proj),
        (pltpu.VMEM(pair.shape, bf16), pltpu.SemaphoreType.DMA),
        in_hbm=(0,),
    )
    crossed = call(
        cross_kernel,
        tuple(sds((group, rows, devices * rows), bf16) for _ in range(blocks)),
        (right, *lefts),
    )
    crossed = exchange(crossed, devices)
    return call(
        final_kernel,
        sds((rows, tokens, width), bf16),
        (me, gate, out_proj, *crossed),
        (
            total,
            pltpu.VMEM((rows, tokens, width), bf16),
            pltpu.SemaphoreType.DMA((tokens // 128,)),
        ),
        out_hbm=True,
    )


def solution(mesh):
    in_specs = (P(("parts", "row"), None, None), P(("parts", "row"), None), P(), P(), P(), P())
    out_specs = P(("parts", "row"), None, None)
    return jax.shard_map(
        functools.partial(on_device, mesh.shape["row"]),
        mesh=mesh, in_specs=in_specs, out_specs=out_specs, check_vma=False,
    )
```

```python
import functools

import jax
import jax.numpy as jnp
from jax import lax
from jax.experimental import pallas as pl
from jax.experimental.pallas import tpu as pltpu
from jax.sharding import PartitionSpec as P

EPS = 1e-05
VMEM = pl.BlockSpec(memory_space=pltpu.VMEM)
SMEM = pl.BlockSpec(memory_space=pltpu.SMEM)
ANY = pl.BlockSpec(memory_space=pl.ANY)
OVER_LAST = (((1,), (1,)), ((), ()))


def steps_of(blocks):
    return (0, 6, 7, 2, 4, 3, 5, 1) if blocks == 8 else tuple(range(blocks))


def sigmoid(x):
    return 0.5 * jnp.tanh(0.5 * x) + 0.5


def normed_rows(pair, gain, mean_by_dot=False):
    x = pair.astype(jnp.float32)
    if mean_by_dot:
        width = pair.shape[1]
        ones = jnp.full((width, width), 1 / width, jnp.bfloat16)
        mean = jnp.dot(pair, ones, preferred_element_type=jnp.float32)
    else:
        mean = jnp.mean(x, axis=-1, keepdims=True)
    centered = x - mean
    variance = jnp.mean(centered * centered, axis=-1, keepdims=True)
    return (centered * lax.rsqrt(variance + EPS) * gain).astype(jnp.bfloat16)


def halved_gates(weights):
    hidden = weights.shape[1] // 2
    return jnp.concatenate([weights[:, :hidden], weights[:, hidden:] * 0.5], axis=1).T


def gated(pair_ref, mask_ref, weights, gain, total, t):
    rows = pair_ref.shape[0]
    hidden = weights.shape[0] // 2
    lanes = slice(t * 128, (t + 1) * 128)
    normed = normed_rows(pair_ref[:, lanes].reshape(rows * 128, -1), gain, mean_by_dot=True)
    proj = lax.dot_general(weights, normed, OVER_LAST, preferred_element_type=jnp.float32)
    for r in range(rows):
        of_row = proj[:, r * 128 : (r + 1) * 128]
        half_keep = 0.5 * mask_ref[r : r + 1, lanes].astype(jnp.float32)
        total[t, pl.ds(r, hidden, stride=rows), :] = (
            (jnp.tanh(of_row[hidden:]) + 1.0) * (of_row[:hidden] * half_keep)
        )


def right_kernel(
    pair_hbm, mask_hbm, gain_hbm, proj_hbm, out_hbm,
    pair_ref, mask_ref, gain_ref, weights_ref, total, staged, in_sems, out_sems,
):
    copies, blocks, group, rows, tokens = out_hbm.shape
    hidden = blocks * group
    chunks = tokens // 128
    loads = [
        pltpu.make_async_copy(
            pair_hbm.at[:, pl.ds(t * 128, 128)], pair_ref.at[:, pl.ds(t * 128, 128)], in_sems.at[t]
        )
        for t in range(chunks)
    ]
    small_loads = [
        pltpu.make_async_copy(source, target, in_sems.at[chunks + i])
        for i, (source, target) in enumerate((
            (proj_hbm.at[:, 2 * hidden : 4 * hidden], weights_ref),
            (mask_hbm, mask_ref),
            (gain_hbm, gain_ref),
        ))
    ]
    for load in loads[:1] + small_loads + loads[1:]:
        load.start()
    for load in small_loads:
        load.wait()
    weights = halved_gates(weights_ref[...])
    gain = gain_ref[...]
    stores = []
    for t in range(chunks):
        lanes = slice(t * 128, (t + 1) * 128)
        loads[t].wait()
        gated(pair_ref, mask_ref, weights, gain, total, t)
        for b in range(blocks):
            block = total[t, b * group * rows : (b + 1) * group * rows, :].astype(jnp.bfloat16)
            staged[b, :, :, lanes] = block.reshape(group, rows, 128)
            part = pl.ds(t * 128, 128)
            for c in range(copies):
                store = pltpu.make_async_copy(
                    staged.at[b, :, :, part], out_hbm.at[c, b, :, :, part], out_sems.at[c, b, t]
                )
                store.start()
                stores.append(store)
    for store in stores:
        store.wait()


def left_kernel(me_ref, pair_ref, mask_ref, gain_ref, proj_ref, *rest):
    *out_refs, total = rest
    blocks = len(out_refs)
    group, rows, tokens = out_refs[0].shape
    weights = halved_gates(proj_ref[:, : 2 * blocks * group])
    gain = gain_ref[...]
    for t in range(tokens // 128):
        gated(pair_ref, mask_ref, weights, gain, total, t)
        for step, out_ref in zip(steps_of(blocks), out_refs):
            first = pl.multiple_of((me_ref[0] ^ step) * (group * rows), group * rows)
            block = total[t, pl.ds(first, group * rows), :].astype(jnp.bfloat16)
            out_ref[:, :, t * 128 : (t + 1) * 128] = block.reshape(group, rows, 128)


def cross_kernel(right_ref, *rest):
    blocks = len(rest) // 2
    left_refs, out_refs = rest[:blocks], rest[blocks:]
    sources, group, rows, tokens = right_ref.shape
    for c in range(group):
        right = right_ref[:, c].reshape(sources * rows, tokens)
        left = jnp.concatenate([ref[c] for ref in left_refs], axis=0)
        crossed = lax.dot_general(left, right, OVER_LAST, preferred_element_type=jnp.float32)
        crossed = crossed.astype(jnp.bfloat16).reshape(blocks, rows, sources * rows)
        for s, out_ref in enumerate(out_refs):
            out_ref[c] = crossed[s]


def gate_kernel(pair_hbm, gain_ref, proj_ref, out_ref, pair_ref, sem):
    load = pltpu.make_async_copy(pair_hbm, pair_ref, sem)
    load.start()
    rows = pair_ref.shape[0]
    gain = gain_ref[...]
    weights = proj_ref[...]
    load.wait()

    def step(r, carry):
        normed = normed_rows(pair_ref[r], gain)
        out_ref[r] = sigmoid(jnp.dot(normed, weights, preferred_element_type=jnp.float32))
        return carry

    lax.fori_loop(0, rows, step, 0, unroll=4)


def final_kernel(me_ref, gate_ref, proj_ref, *rest):
    *crossed_refs, out_hbm, total, staged, sems = rest
    group, rows, tokens = crossed_refs[0].shape
    hidden = group * len(crossed_refs)
    weights = proj_ref[...]
    stores = []
    for t in range(tokens // 128):
        lanes = slice(t * 128, (t + 1) * 128)
        x = jnp.concatenate([ref[:, :, lanes] for ref in crossed_refs], axis=0)
        x = x.astype(jnp.float32)
        centered = x - jnp.mean(x, axis=0, keepdims=True)
        variance = jnp.mean(centered * centered, axis=0, keepdims=True)
        x = (centered * lax.rsqrt(variance + EPS)).reshape(len(crossed_refs), group * rows, 128)
        for s, step in enumerate(steps_of(len(crossed_refs))):
            owner = me_ref[0] ^ step
            first = pl.multiple_of(owner * (group * rows), group * rows)
            total[t, pl.ds(first, group * rows), :] = x[s]
        for r in range(rows):
            x = total[t, pl.ds(r, hidden, stride=rows), :].T.astype(jnp.bfloat16)
            mixed = jnp.dot(x, weights, preferred_element_type=jnp.float32)
            staged[r, lanes, :] = (gate_ref[r, lanes, :] * mixed).astype(jnp.bfloat16)
        part = pl.ds(t * 128, 128)
        store = pltpu.make_async_copy(staged.at[:, part], out_hbm.at[:, part], sems.at[t])
        store.start()
        stores.append(store)
    for store in stores:
        store.wait()


def call(kernel, out_shape, operands, scratch=(), in_hbm=(), out_hbm=False, limit=48, cost=1.0):
    specs = [
        ANY if i in in_hbm else SMEM if x.ndim == 1 else VMEM
        for i, x in enumerate(operands)
    ]
    return pl.pallas_call(
        kernel,
        out_shape=out_shape,
        in_specs=specs,
        out_specs=jax.tree.map(lambda _: ANY if out_hbm else VMEM, out_shape),
        scratch_shapes=list(scratch),
        compiler_params=pltpu.CompilerParams(vmem_limit_bytes=limit * 2**20),
        cost_estimate=pl.CostEstimate(
            flops=int(cost * 1e9), bytes_accessed=int(cost * 4e6), transcendentals=0
        ),
    )(*operands)


def exchange(parts, devices):
    return [
        lax.ppermute(part, "row", [(i, i ^ step) for i in range(devices)]) if step else part
        for part, step in zip(parts, steps_of(len(parts)))
    ]


def on_device(devices, pair, pair_mask, in_gain, in_proj, gate_proj, out_proj):
    rows, tokens, width = pair.shape
    hidden = out_proj.shape[0]
    blocks = devices // 2
    group = hidden // blocks
    sds = jax.ShapeDtypeStruct
    bf16 = jnp.bfloat16
    me = lax.rem(lax.axis_index("row"), blocks).astype(jnp.int32).reshape(1)
    gain = in_gain.reshape(1, width)
    total = pltpu.VMEM((tokens // 128, (hidden + 1) * rows, 128), jnp.float32)

    right = call(
        right_kernel,
        sds((2, blocks, group, rows, tokens), bf16),
        (pair, pair_mask, gain, in_proj),
        (
            pltpu.VMEM(pair.shape, bf16),
            pltpu.VMEM(pair_mask.shape, jnp.int32),
            pltpu.VMEM(gain.shape, jnp.float32),
            pltpu.VMEM((width, 2 * hidden), bf16),
            total,
            pltpu.VMEM((blocks, group, rows, tokens), bf16),
            pltpu.SemaphoreType.DMA((tokens // 128 + 3,)),
            pltpu.SemaphoreType.DMA((2, blocks, tokens // 128)),
        ),
        in_hbm=range(4),
        out_hbm=True,
        limit=62,
    ).reshape(devices, group, rows, tokens)
    right = lax.all_to_all(right, "row", split_axis=0, concat_axis=0, tiled=True)
    lefts = call(
        left_kernel,
        tuple(sds((group, rows, tokens), bf16) for _ in range(blocks)),
        (me, pair, pair_mask, gain, in_proj),
        (total,),
    )
    lefts = exchange(lefts, devices)
    gate = call(
        gate_kernel,
        sds((rows, tokens, width), jnp.float32),
        (pltpu.with_memory_space_constraint(pair, pltpu.HBM), gain, gate_proj),
        (pltpu.VMEM(pair.shape, bf16), pltpu.SemaphoreType.DMA),
        in_hbm=(0,),
    )
    crossed = call(
        cross_kernel,
        tuple(sds((group, rows, devices * rows), bf16) for _ in range(blocks)),
        (right, *lefts),
    )
    crossed = exchange(crossed, devices)
    return call(
        final_kernel,
        sds((rows, tokens, width), bf16),
        (me, gate, out_proj, *crossed),
        (
            total,
            pltpu.VMEM((rows, tokens, width), bf16),
            pltpu.SemaphoreType.DMA((tokens // 128,)),
        ),
        out_hbm=True,
    )


def solution(mesh):
    in_specs = (P(("parts", "row"), None, None), P(("parts", "row"), None), P(), P(), P(), P())
    out_specs = P(("parts", "row"), None, None)
    return jax.shard_map(
        functools.partial(on_device, mesh.shape["row"]),
        mesh=mesh, in_specs=in_specs, out_specs=out_specs, check_vma=False,
    )
```

```python
import functools

import jax
import jax.numpy as jnp
from jax import lax
from jax.experimental import pallas as pl
from jax.experimental.pallas import tpu as pltpu
from jax.sharding import PartitionSpec as P

EPS = 1e-05
VMEM = pl.BlockSpec(memory_space=pltpu.VMEM)
SMEM = pl.BlockSpec(memory_space=pltpu.SMEM)
ANY = pl.BlockSpec(memory_space=pl.ANY)
OVER_LAST = (((1,), (1,)), ((), ()))


def steps_of(blocks):
    return (0, 1, 6, 2, 4, 7, 3, 5) if blocks == 8 else tuple(range(blocks))


def back_of(blocks):
    return (0, 6, 2, 4, 3, 5, 7, 1) if blocks == 8 else tuple(range(blocks))


def sigmoid(x):
    return 0.5 * jnp.tanh(0.5 * x) + 0.5


def normed_rows(pair, gain, mean_by_dot=False):
    x = pair.astype(jnp.float32)
    if mean_by_dot:
        width = pair.shape[1]
        ones = jnp.full((width, width), 1 / width, jnp.bfloat16)
        mean = jnp.dot(pair, ones, preferred_element_type=jnp.float32)
    else:
        mean = jnp.mean(x, axis=-1, keepdims=True)
    centered = x - mean
    variance = jnp.mean(centered * centered, axis=-1, keepdims=True)
    return (centered * lax.rsqrt(variance + EPS) * gain).astype(jnp.bfloat16)


def halved_gates(weights):
    hidden = weights.shape[1] // 2
    return jnp.concatenate([weights[:, :hidden], weights[:, hidden:] * 0.5], axis=1).T


def gated(pair_ref, mask_ref, weights, gain, total, t):
    rows = pair_ref.shape[0]
    hidden = weights.shape[0] // 2
    lanes = slice(t * 128, (t + 1) * 128)
    normed = normed_rows(pair_ref[:, lanes].reshape(rows * 128, -1), gain, mean_by_dot=True)
    proj = lax.dot_general(weights, normed, OVER_LAST, preferred_element_type=jnp.float32)
    for r in range(rows):
        of_row = proj[:, r * 128 : (r + 1) * 128]
        half_keep = 0.5 * mask_ref[r : r + 1, lanes].astype(jnp.float32)
        total[t, pl.ds(r, hidden, stride=rows), :] = (
            (jnp.tanh(of_row[hidden:]) + 1.0) * (of_row[:hidden] * half_keep)
        )


def right_kernel(
    pair_hbm, mask_hbm, gain_hbm, proj_hbm, out_hbm,
    pair_ref, mask_ref, gain_ref, weights_ref, total, staged, in_sems, out_sems,
):
    copies, blocks, group, rows, tokens = out_hbm.shape
    hidden = blocks * group
    chunks = tokens // 128
    loads = [
        pltpu.make_async_copy(
            pair_hbm.at[:, pl.ds(t * 128, 128)], pair_ref.at[:, pl.ds(t * 128, 128)], in_sems.at[t]
        )
        for t in range(chunks)
    ]
    small_loads = [
        pltpu.make_async_copy(source, target, in_sems.at[chunks + i])
        for i, (source, target) in enumerate((
            (proj_hbm.at[:, 2 * hidden : 4 * hidden], weights_ref),
            (mask_hbm, mask_ref),
            (gain_hbm, gain_ref),
        ))
    ]
    for load in loads[:1] + small_loads + loads[1:]:
        load.start()
    for load in small_loads:
        load.wait()
    weights = halved_gates(weights_ref[...])
    gain = gain_ref[...]
    stores = []
    for t in range(chunks):
        lanes = slice(t * 128, (t + 1) * 128)
        loads[t].wait()
        gated(pair_ref, mask_ref, weights, gain, total, t)
        for b in range(blocks):
            block = total[t, b * group * rows : (b + 1) * group * rows, :].astype(jnp.bfloat16)
            staged[b, :, :, lanes] = block.reshape(group, rows, 128)
            part = pl.ds(t * 128, 128)
            for c in range(copies):
                store = pltpu.make_async_copy(
                    staged.at[b, :, :, part], out_hbm.at[c, b, :, :, part], out_sems.at[c, b, t]
                )
                store.start()
                stores.append(store)
    for store in stores:
        store.wait()


def left_kernel(me_ref, pair_ref, mask_ref, gain_ref, proj_ref, *rest):
    *out_refs, total = rest
    blocks = len(out_refs)
    group, rows, tokens = out_refs[0].shape
    weights = halved_gates(proj_ref[:, : 2 * blocks * group])
    gain = gain_ref[...]
    for t in range(tokens // 128):
        gated(pair_ref, mask_ref, weights, gain, total, t)
        for step, out_ref in zip(steps_of(blocks), out_refs):
            first = pl.multiple_of((me_ref[0] ^ step) * (group * rows), group * rows)
            block = total[t, pl.ds(first, group * rows), :].astype(jnp.bfloat16)
            out_ref[:, :, t * 128 : (t + 1) * 128] = block.reshape(group, rows, 128)


def cross_kernel(right_ref, *rest):
    blocks = len(rest) // 2
    left_refs, out_refs = rest[:blocks], rest[blocks:]
    sources, group, rows, tokens = right_ref.shape
    for c in range(group):
        right = right_ref[:, c].reshape(sources * rows, tokens)
        left = jnp.concatenate([ref[c] for ref in left_refs], axis=0)
        crossed = lax.dot_general(left, right, OVER_LAST, preferred_element_type=jnp.float32)
        crossed = crossed.astype(jnp.bfloat16).reshape(blocks, rows, sources * rows)
        for step, out_ref in zip(back_of(blocks), out_refs):
            out_ref[c] = crossed[steps_of(blocks).index(step)]


def gate_kernel(pair_hbm, gain_ref, proj_ref, out_ref, pair_ref, sem):
    load = pltpu.make_async_copy(pair_hbm, pair_ref, sem)
    load.start()
    rows = pair_ref.shape[0]
    gain = gain_ref[...]
    weights = proj_ref[...]
    load.wait()

    def step(r, carry):
        normed = normed_rows(pair_ref[r], gain)
        out_ref[r] = sigmoid(jnp.dot(normed, weights, preferred_element_type=jnp.float32))
        return carry

    lax.fori_loop(0, rows, step, 0, unroll=4)


def final_kernel(me_ref, gate_ref, proj_ref, *rest):
    *crossed_refs, out_hbm, total, staged, sems = rest
    group, rows, tokens = crossed_refs[0].shape
    hidden = group * len(crossed_refs)
    weights = proj_ref[...]
    stores = []
    for t in range(tokens // 128):
        lanes = slice(t * 128, (t + 1) * 128)
        x = jnp.concatenate([ref[:, :, lanes] for ref in crossed_refs], axis=0)
        x = x.astype(jnp.float32)
        centered = x - jnp.mean(x, axis=0, keepdims=True)
        variance = jnp.mean(centered * centered, axis=0, keepdims=True)
        x = (centered * lax.rsqrt(variance + EPS)).reshape(len(crossed_refs), group * rows, 128)
        for s, step in enumerate(back_of(len(crossed_refs))):
            owner = me_ref[0] ^ step
            first = pl.multiple_of(owner * (group * rows), group * rows)
            total[t, pl.ds(first, group * rows), :] = x[s]
        for r in range(rows):
            x = total[t, pl.ds(r, hidden, stride=rows), :].T.astype(jnp.bfloat16)
            mixed = jnp.dot(x, weights, preferred_element_type=jnp.float32)
            staged[r, lanes, :] = (gate_ref[r, lanes, :] * mixed).astype(jnp.bfloat16)
        part = pl.ds(t * 128, 128)
        store = pltpu.make_async_copy(staged.at[:, part], out_hbm.at[:, part], sems.at[t])
        store.start()
        stores.append(store)
    for store in stores:
        store.wait()


def call(kernel, out_shape, operands, scratch=(), in_hbm=(), out_hbm=False, limit=48, cost=1.0):
    specs = [
        ANY if i in in_hbm else SMEM if x.ndim == 1 else VMEM
        for i, x in enumerate(operands)
    ]
    return pl.pallas_call(
        kernel,
        out_shape=out_shape,
        in_specs=specs,
        out_specs=jax.tree.map(lambda _: ANY if out_hbm else VMEM, out_shape),
        scratch_shapes=list(scratch),
        compiler_params=pltpu.CompilerParams(vmem_limit_bytes=limit * 2**20),
        cost_estimate=pl.CostEstimate(
            flops=int(cost * 1e9), bytes_accessed=int(cost * 4e6), transcendentals=0
        ),
    )(*operands)


def exchange(parts, devices, steps_of=steps_of):
    return [
        lax.ppermute(part, "row", [(i, i ^ step) for i in range(devices)]) if step else part
        for part, step in zip(parts, steps_of(len(parts)))
    ]


def on_device(devices, pair, pair_mask, in_gain, in_proj, gate_proj, out_proj):
    rows, tokens, width = pair.shape
    hidden = out_proj.shape[0]
    blocks = devices // 2
    group = hidden // blocks
    sds = jax.ShapeDtypeStruct
    bf16 = jnp.bfloat16
    me = lax.rem(lax.axis_index("row"), blocks).astype(jnp.int32).reshape(1)
    gain = in_gain.reshape(1, width)
    total = pltpu.VMEM((tokens // 128, (hidden + 1) * rows, 128), jnp.float32)

    right = call(
        right_kernel,
        sds((2, blocks, group, rows, tokens), bf16),
        (pair, pair_mask, gain, in_proj),
        (
            pltpu.VMEM(pair.shape, bf16),
            pltpu.VMEM(pair_mask.shape, jnp.int32),
            pltpu.VMEM(gain.shape, jnp.float32),
            pltpu.VMEM((width, 2 * hidden), bf16),
            total,
            pltpu.VMEM((blocks, group, rows, tokens), bf16),
            pltpu.SemaphoreType.DMA((tokens // 128 + 3,)),
            pltpu.SemaphoreType.DMA((2, blocks, tokens // 128)),
        ),
        in_hbm=range(4),
        out_hbm=True,
        limit=62,
    ).reshape(devices, group, rows, tokens)
    right = lax.all_to_all(right, "row", split_axis=0, concat_axis=0, tiled=True)
    lefts = call(
        left_kernel,
        tuple(sds((group, rows, tokens), bf16) for _ in range(blocks)),
        (me, pair, pair_mask, gain, in_proj),
        (total,),
    )
    lefts = exchange(lefts, devices)
    gate = call(
        gate_kernel,
        sds((rows, tokens, width), jnp.float32),
        (pltpu.with_memory_space_constraint(pair, pltpu.HBM), gain, gate_proj),
        (pltpu.VMEM(pair.shape, bf16), pltpu.SemaphoreType.DMA),
        in_hbm=(0,),
    )
    crossed = call(
        cross_kernel,
        tuple(sds((group, rows, devices * rows), bf16) for _ in range(blocks)),
        (right, *lefts),
    )
    crossed = exchange(crossed, devices, back_of)
    return call(
        final_kernel,
        sds((rows, tokens, width), bf16),
        (me, gate, out_proj, *crossed),
        (
            total,
            pltpu.VMEM((rows, tokens, width), bf16),
            pltpu.SemaphoreType.DMA((tokens // 128,)),
        ),
        out_hbm=True,
    )


def solution(mesh):
    in_specs = (P(("parts", "row"), None, None), P(("parts", "row"), None), P(), P(), P(), P())
    out_specs = P(("parts", "row"), None, None)
    return jax.shard_map(
        functools.partial(on_device, mesh.shape["row"]),
        mesh=mesh, in_specs=in_specs, out_specs=out_specs, check_vma=False,
    )
```
